32 devices in a mesh: replica: 8 (over y, x, core), fsdp: 4 (over z).
Axes of the slice: x: 2, y: 2, z: 4, core: 2. Of those that a mesh axis runs over, the one named last changes fastest.
Arguments:
- activations: bfloat16 [8192, 4096], P(('replica', 'fsdp')), may hold values from -6 to 6
- output_grads: bfloat16 [8192, 512], P(('replica', 'fsdp')), may hold values from -0.1875 to 0.1875
- momentum: bfloat16 [8, 4096, 512], P('replica', 'fsdp'), may hold values from -6 to 6
- chosen_blocks: int32 [8, 64, 8], P('replica', 'fsdp'), may hold values from 0 to 255, as said below
Outputs:
- momentum_next: bfloat16 [8, 4096, 512], P('replica', 'fsdp')
- update: float32 [4096, 512], P('fsdp')
The draws below stay inside these ranges and needn't reach their ends.
Inputs may be any that keep to these rules, and one draw needn't show every extreme that they name: `chosen_blocks`: the 8 numbers of each span row of each replica are different block numbers.
All inputs are finite; a program needn't handle non-finite values.
Results may differ from the reference program's by a relative error of at most 0.013.
Values may be sent and summed in bfloat16 or wider, within the bound.
No kernel may reach another device: no remote copies, remote signals or barrier semaphores. Data moves between devices by JAX's collectives and lax.ppermute only.
A program may use at most 64 MiB of HBM per device.

```python
import jax
import jax.numpy as jnp
from jax import lax

DW = 4096
FW = 512
TOK_DEV = 256
SPAN = 64
BLOCK = 128
TOP = 8
REPLICAS = 8
TOKENS = 8192
CROWS = 64
BLOCKS = 256
N_FSDP = 4


def draw_chosen_blocks(key, part):
    scores = jax.random.randint(key, (REPLICAS, CROWS, BLOCKS), 0, 1 << 20, dtype=jnp.int32)
    scores = scores * BLOCKS + jnp.arange(BLOCKS, dtype=jnp.int32)[None, None, :]
    order = jnp.argsort(scores, axis=-1, stable=True)
    return order[:, :, :TOP].astype(jnp.int32)


def levels(key, shape, shards, smallest, high):
    factor_of, own = 1.0, jax.random.fold_in(key, 6)
    for dim, parts in shards:
        draws = jnp.exp(jax.random.uniform(jax.random.fold_in(own, dim), (parts,), jnp.float32, smallest / len(shards), high / len(shards)))
        factor_of = factor_of * jnp.repeat(draws, shape[dim] // parts).reshape([-1 if axis == dim else 1 for axis in range(len(shape))])
    return factor_of


def bell_draw(stream_key, dims, deviation, reach, pieces=(), held_as=jnp.bfloat16):
    drawn = deviation * jax.random.normal(stream_key, dims, jnp.float32)
    if pieces:
        drawn = drawn * levels(stream_key, dims, pieces, -0.22, 0.18)
    return jnp.clip(drawn, -reach, reach).astype(held_as)


def setup_inputs(seed: int = 0) -> dict:
    splits = jax.random.split(jax.random.key(seed), 5)
    return {
        "activations": bell_draw(splits[0], (TOKENS, DW), 1.0, 6.0, ((0, 32),)),
        "output_grads": bell_draw(splits[1], (TOKENS, FW), (0.5 / TOK_DEV ** 0.5), 0.1875, ((0, 32),)),
        "momentum": bell_draw(splits[2], (REPLICAS, DW, FW), 1.0, 6.0, ((0, 8), (1, 4))),
        "chosen_blocks": draw_chosen_blocks(jax.random.fold_in(splits[4], 71), 0),
    }


def cosine_table():
    order = jnp.arange(SPAN, dtype=jnp.float32)
    freq = order[:, None]
    place = order[None, :]
    factor = jnp.where(freq == 0.0, jnp.sqrt(jnp.float32(1.0 / SPAN)), jnp.sqrt(jnp.float32(2.0 / SPAN)))
    return factor * jnp.cos(jnp.float32(jnp.pi) * (2.0 * place + 1.0) * freq / (2.0 * SPAN))

def forward_blocks(field, table):
    rows = field.shape[0] // SPAN
    cols = field.shape[1] // SPAN
    shaped = field.reshape(rows, SPAN, cols, SPAN)
    coeffs = jnp.einsum('pu,cujv,qv->cjpq', table, shaped, table, precision=lax.Precision.HIGHEST)
    return coeffs.reshape(rows, cols * (SPAN * SPAN // BLOCK), BLOCK)

def inverse_blocks(coeffs, table):
    rows = coeffs.shape[0]
    cols = coeffs.shape[1] * BLOCK // (SPAN * SPAN)
    shaped = coeffs.reshape(rows, cols, SPAN, SPAN)
    field = jnp.einsum('pu,cjpq,qv->cujv', table, shaped, table, precision=lax.Precision.HIGHEST)
    return field.reshape(rows * SPAN, cols * SPAN)

def reference(activations, output_grads, momentum, chosen_blocks):
    table = cosine_table()
    xs = activations.reshape(REPLICAS, N_FSDP, TOK_DEV, DW)
    gs = output_grads.reshape(REPLICAS, N_FSDP, TOK_DEV, FW)
    numbers = jnp.arange(BLOCKS, dtype=jnp.int32)

    def one_replica(total, items):
        inputs, grads, moment_old, picks = items
        partial_terms = jnp.einsum('ftd,ftg->fdg', inputs.astype(jnp.float32), grads.astype(jnp.float32))
        rounded = lax.optimization_barrier(partial_terms.astype(jnp.bfloat16))
        grad = lax.optimization_barrier(jnp.sum(rounded.astype(jnp.float32), axis=0))
        moment = 0.9 * moment_old.astype(jnp.float32) + grad
        coeffs = forward_blocks(moment, table)
        mask = lax.optimization_barrier(jnp.sum((picks[:, :, None] == numbers[None, None, :]).astype(jnp.float32), axis=1))
        sent = lax.optimization_barrier((coeffs * mask[:, :, None]).astype(jnp.bfloat16))
        kept = coeffs * (1.0 - mask[:, :, None])
        moment_next = inverse_blocks(kept, table).astype(jnp.bfloat16)
        return (total + sent.astype(jnp.float32), moment_next)
    start = jnp.zeros((CROWS, BLOCKS, BLOCK), jnp.float32)
    total, momentum_next = lax.scan(one_replica, start, (xs, gs, momentum, chosen_blocks))
    update = inverse_blocks(total, table)
    return (momentum_next, update)
```

```python
import functools

import jax
import jax.numpy as jnp
import numpy as np
from jax import lax
from jax.experimental import pallas as pl
from jax.experimental.pallas import tpu as pltpu
from jax.sharding import PartitionSpec as P

F32 = jnp.float32
BF16 = jnp.bfloat16
SIZE = 64
LANES = 128
GROUP = 4


def table_parts():
    order = np.arange(SIZE, dtype=np.float64)[:, None]
    place = np.arange(SIZE, dtype=np.float64)[None, :]
    factor = np.where(order == 0, np.sqrt(1.0 / SIZE), np.sqrt(2.0 / SIZE))
    table = factor * np.cos(np.pi * (2 * place + 1) * order / (2 * SIZE))
    high = table.astype(jnp.bfloat16)
    low = (table - high.astype(np.float64)).astype(jnp.bfloat16)
    return high, low


def dot(a, b):
    return lax.dot_general(a, b, (((1,), (0,)), ((), ())), preferred_element_type=F32)


def dot_nt(a, b):
    return lax.dot_general(a, b, (((1,), (1,)), ((), ())), preferred_element_type=F32)


def dot_tn(a, b):
    return lax.dot_general(a, b, (((0,), (0,)), ((), ())), preferred_element_type=F32)


def split(x):
    high = x.astype(BF16)
    return high, (x - high.astype(F32)).astype(BF16)


def iota(shape, dim):
    return lax.broadcasted_iota(jnp.int32, shape, dim)


def choice(picks, top):
    crows = picks.shape[0]
    rows = crows * top * 2
    r1 = iota((rows, crows), 0)
    owner = GROUP * (r1 // (2 * GROUP * top)) + (r1 // top) % GROUP
    spread = (iota((rows, crows), 1) == owner).astype(F32).astype(BF16)
    r2 = iota((rows, LANES), 0)
    numbers = jnp.where(iota((rows, LANES), 1) == r2 % top, dot(spread, picks), 0.0)
    number = jnp.sum(numbers, axis=1, keepdims=True).astype(jnp.int32)
    half = (iota((rows, 1), 0) // (GROUP * top)) % 2
    return number // (SIZE // 2), 2 * (number % (SIZE // 2)) + half


def onehot(order):
    rows = order.shape[0]
    return (iota((rows, SIZE), 1) == order).astype(F32).astype(BF16)


def chosen_rows(order, top, c4h, c4l):
    rows = order.shape[0]
    hot = onehot(order)
    own = (iota((rows, GROUP * SIZE), 1) // SIZE) == ((iota((rows, GROUP * SIZE), 0) // top) % GROUP)
    high = jnp.where(own, dot(hot, c4h), 0.0).astype(BF16)
    low = jnp.where(own, dot(hot, c4l), 0.0).astype(BF16)
    return high, low


def span_mask(span, width):
    rows = span.shape[0]
    return (iota((rows, width), 1) // SIZE) == span


def forward_cols(masked, csth, cstl):
    high, low = split(masked)
    return dot_nt(high, csth) + dot_nt(low, csth) + dot_nt(high, cstl)


def pack_halves(v, top):
    step = GROUP * top
    parts = []
    for g in range(v.shape[0] // (2 * step)):
        a = v[2 * g * step : (2 * g + 1) * step]
        b = v[(2 * g + 1) * step : (2 * g + 2) * step]
        parts.append(jnp.concatenate([a, b], axis=1))
    return jnp.concatenate(parts, axis=0)


def chosen_kernel(top, me_ref, picks_ref, acts_ref, g_ref, m_ref, c4h_ref, c4l_ref, csth_ref, cstl_ref,
                  own_ref, o1_ref, o2_ref, o3_ref):
    me = me_ref[0]
    shard = m_ref.shape[0]
    width = m_ref.shape[1]
    crows = shard // SIZE
    groups = crows // GROUP
    c4h, c4l = c4h_ref[...], c4l_ref[...]
    csth, cstl = csth_ref[...], cstl_ref[...]
    gmat = g_ref[...]
    outs = (own_ref, o1_ref, o2_ref, o3_ref)
    for s in range(4):
        target = me ^ s
        span, order = choice(picks_ref[s * crows : (s + 1) * crows, :], top)
        high, low = chosen_rows(order, top, c4h, c4l)
        step = 2 * GROUP * top
        parts = []
        for g in range(groups):
            start = pl.multiple_of(target * shard + g * GROUP * SIZE, GROUP * SIZE)
            block = acts_ref[:, pl.ds(start, GROUP * SIZE)]
            both = jnp.concatenate([high[g * step : (g + 1) * step], low[g * step : (g + 1) * step]], axis=0)
            t = dot_nt(both, block)
            parts.append(t[:step] + t[step:])
        th, tl = split(jnp.concatenate(parts, axis=0))
        a = dot(th, gmat) + dot(tl, gmat)
        if s == 0:
            parts = []
            for g in range(groups):
                block = m_ref[g * GROUP * SIZE : (g + 1) * GROUP * SIZE, :]
                parts.append(
                    dot(high[g * step : (g + 1) * step], block) + dot(low[g * step : (g + 1) * step], block)
                )
            a = a + 0.9 * jnp.concatenate(parts, axis=0)
        v = forward_cols(jnp.where(span_mask(span, width), a, 0.0), csth, cstl)
        outs[s][...] = pack_halves(v, top).astype(outs[s].dtype)


def base_kernel(top, picks_ref, v_ref, m_ref, a0_ref, ao_ref, g_ref, gp_ref, c4th_ref, c4tl_ref, csth_ref, cstl_ref,
                out_ref):
    shard, width = m_ref.shape
    crows = shard // SIZE
    groups = crows // GROUP
    step = GROUP * top
    span, order = choice(picks_ref[...], top)
    hot = onehot(order)
    v = v_ref[...]
    parts = []
    for g in range(groups):
        block = v[g * step : (g + 1) * step]
        parts += [block[:, :SIZE], block[:, SIZE:]]
    vh, vl = split(jnp.concatenate(parts, axis=0))
    csth, cstl = csth_ref[...], cstl_ref[...]
    x = dot(vh, csth) + dot(vl, csth) + dot(vh, cstl)
    xh, xl = split(jnp.where(span_mask(span, width), x, 0.0))
    gmat, gpmat = g_ref[...], gp_ref[...]
    rows = GROUP * SIZE
    own = (iota((rows, 2 * step), 0) // SIZE) == ((iota((rows, 2 * step), 1) // top) % GROUP)
    for g in range(groups):
        here = slice(g * 2 * step, (g + 1) * 2 * step)
        th = jnp.where(own, dot_nt(c4th_ref[...], hot[here]), 0.0).astype(BF16)
        tl = jnp.where(own, dot_nt(c4tl_ref[...], hot[here]), 0.0).astype(BF16)
        inv = dot(th, xh[here]) + dot(tl, xh[here]) + dot(th, xl[here])
        at = slice(g * rows, (g + 1) * rows)
        pair = dot_tn(a0_ref[:, at], gmat) + dot_tn(ao_ref[:, at], gpmat)
        out_ref[at, :] = 0.9 * m_ref[at, :].astype(F32) + pair - inv


def update_kernel(top, crows, pack_ref, c2th_ref, c2tl_ref, csth_ref, cstl_ref, out_ref, xh_ref, xl_ref):
    reps = pack_ref.shape[0]
    width = out_ref.shape[1]
    per = crows * top

    @pl.when(pl.program_id(0) == 0)
    def _():
        out_ref[...] = jnp.zeros_like(out_ref)

    r1 = iota((per, crows), 0)
    spread = (iota((per, crows), 1) == r1 // top).astype(F32).astype(BF16)
    pickmask = iota((per, LANES), 1) == iota((per, LANES), 0) % top
    csth, cstl = csth_ref[...], cstl_ref[...]
    zero = jnp.zeros_like(csth)
    numbers = []
    for r in range(reps):
        v = pack_ref[r, :per, :]
        picks = pack_ref[r, per : per + crows, :]
        number = jnp.sum(jnp.where(pickmask, dot(spread, picks), 0.0), axis=1, keepdims=True).astype(jnp.int32)
        numbers.append(number)
        mask = span_mask(number // (SIZE // 2), width)
        for p in range(2):
            wh = jnp.concatenate([csth, zero] if p == 0 else [zero, csth], axis=0)
            wl = jnp.concatenate([cstl, zero] if p == 0 else [zero, cstl], axis=0)
            xh, xl = split(jnp.where(mask, dot(v, wh) + dot(v, wl), 0.0))
            xh_ref[p, r] = xh
            xl_ref[p, r] = xl
    pair = 2 * top
    cols = 2 * reps * pair
    rows = 2 * SIZE
    own = (iota((rows, cols), 0) // SIZE) == ((iota((rows, cols), 1) // top) % 2)
    for g in range(crows // 2):
        at = slice(g * pair, (g + 1) * pair)
        bh = jnp.concatenate([xh_ref[p, r, at, :] for p in range(2) for r in range(reps)], axis=0)
        bl = jnp.concatenate([xl_ref[p, r, at, :] for p in range(2) for r in range(reps)], axis=0)
        order = jnp.concatenate(
            [2 * (numbers[r][at] % (SIZE // 2)) + p for p in range(2) for r in range(reps)], axis=0
        )
        hot = onehot(order)
        th = jnp.where(own, dot_nt(c2th_ref[...], hot), 0.0).astype(BF16)
        tl = jnp.where(own, dot_nt(c2tl_ref[...], hot), 0.0).astype(BF16)
        out_ref[g * rows : (g + 1) * rows, :] += dot(th, bh) + dot(tl, bh) + dot(th, bl)


VMEM = functools.partial(pl.BlockSpec, memory_space=pltpu.VMEM)
PARAMS = pltpu.CompilerParams(vmem_limit_bytes=32 * 1024 * 1024)


def swap(x, bit, axis, size):
    return lax.ppermute(x, axis, [(i, i ^ bit) for i in range(size)])


def gather_replicas(x, replicas):
    if replicas & (replicas - 1):
        return lax.all_gather(x, "replica", axis=0, tiled=False)
    stack, bit = x[None], 1
    while bit < replicas:
        stack = jnp.concatenate([stack, swap(stack, bit, "replica", replicas)], axis=0)
        bit *= 2
    return stack


def body(replicas, fsdp, activations, output_grads, momentum, chosen_blocks):
    old = momentum[0]
    shard, width = old.shape
    tokens = activations.shape[0]
    crows = shard // SIZE
    top = chosen_blocks.shape[2]
    chunks = 4
    rows = shard // chunks
    spans = width // SIZE
    high, low = table_parts()
    c4h, c4l = (np.tile(t, (1, GROUP)) for t in (high, low))
    c4th, c4tl = (np.tile(t.T, (GROUP, 1)) for t in (high, low))
    c2th, c2tl = (np.tile(t.T, (2, 1)) for t in (high, low))
    csth, cstl = (np.tile(t, (1, spans)) for t in (high, low))
    me = lax.axis_index("fsdp")

    partner_grads = swap(output_grads, 1, "fsdp", fsdp)
    picks = jnp.pad(chosen_blocks[0].astype(BF16), ((0, 0), (0, LANES - top)))

    def columns(s, start, size):
        return lax.dynamic_slice(activations, (0, (me ^ s) * shard + start), (tokens, size))

    partner_cols = [swap(columns(3, i * rows, rows), 1, "fsdp", fsdp) for i in range(chunks)]
    picks2 = jnp.concatenate([picks, swap(picks, 1, "fsdp", fsdp)], axis=0)
    picks4 = jnp.concatenate([picks2, swap(picks2, 2, "fsdp", fsdp)], axis=0)
    partner_own = swap(columns(1, 0, shard), 1, "fsdp", fsdp)

    vals = jax.ShapeDtypeStruct((crows * top, 2 * SIZE), BF16)
    v0, v1, v2, v3 = pl.pallas_call(
        functools.partial(chosen_kernel, top),
        out_shape=[jax.ShapeDtypeStruct((crows * top, 2 * SIZE), F32), vals, vals, vals],
        in_specs=[pl.BlockSpec(memory_space=pltpu.SMEM)] + [VMEM()] * 8,
        out_specs=[VMEM()] * 4,
        compiler_params=PARAMS,
        name="chosen",
    )(jnp.reshape(me, (1,)), picks4, activations, output_grads, old, c4h, c4l, csth, cstl)
    from_partner = swap(jnp.concatenate([v1, v3], axis=0), 1, "fsdp", fsdp)
    own_pair = v0 + from_partner[: crows * top].astype(F32)
    far_pair = (v2.astype(F32) + from_partner[crows * top :].astype(F32)).astype(BF16)
    values = own_pair + swap(far_pair, 2, "fsdp", fsdp).astype(F32)
    pack = jnp.concatenate([values.astype(BF16), picks], axis=0)

    sums = []
    for i in range(chunks):
        s = dot_tn(columns(2, i * rows, rows), output_grads) + dot_tn(partner_cols[i], partner_grads)
        sums.append(swap(s.astype(BF16), 2, "fsdp", fsdp))

    base = pl.pallas_call(
        functools.partial(base_kernel, top),
        out_shape=jax.ShapeDtypeStruct((shard, width), F32),
        in_specs=[VMEM()] * 11,
        out_specs=VMEM(),
        compiler_params=PARAMS,
        name="base",
    )(picks, values, old, columns(0, 0, shard), partner_own, output_grads, partner_grads, c4th, c4tl, csth, cstl)

    everyone = gather_replicas(pack, replicas)
    step = 8 if replicas % 8 == 0 else 1
    update = pl.pallas_call(
        functools.partial(update_kernel, top, crows),
        grid=(replicas // step,),
        out_shape=jax.ShapeDtypeStruct((shard, width), F32),
        in_specs=[pl.BlockSpec((step, pack.shape[0], LANES), lambda i: (i, 0, 0))] + [VMEM()] * 4,
        out_specs=pl.BlockSpec((shard, width), lambda i: (0, 0)),
        scratch_shapes=[pltpu.VMEM((2, step, crows * top, width), BF16)] * 2,
        compiler_params=PARAMS,
        name="update",
    )(everyone, c2th, c2tl, csth, cstl)
    moment_next = (base + jnp.concatenate(sums, axis=0).astype(F32)).astype(BF16)
    return moment_next[None], update


def solution(mesh):
    return jax.shard_map(
        functools.partial(body, mesh.shape["replica"], mesh.shape["fsdp"]),
        mesh=mesh,
        in_specs=(
            P(("replica", "fsdp"), None),
            P(("replica", "fsdp"), None),
            P("replica", "fsdp", None),
            P("replica", "fsdp", None),
        ),
        out_specs=(P("replica", "fsdp", None), P("fsdp", None)),
        check_vma=False,
    )
```

```python
import functools

import jax
import jax.numpy as jnp
import numpy as np
from jax import lax
from jax.experimental import pallas as pl
from jax.experimental.pallas import tpu as pltpu
from jax.sharding import PartitionSpec as P

F32 = jnp.float32
BF16 = jnp.bfloat16
SIZE = 64
LANES = 128
GATHER = True
GROUP = 4


def table_parts():
    order = np.arange(SIZE, dtype=np.float64)[:, None]
    place = np.arange(SIZE, dtype=np.float64)[None, :]
    factor = np.where(order == 0, np.sqrt(1.0 / SIZE), np.sqrt(2.0 / SIZE))
    table = factor * np.cos(np.pi * (2 * place + 1) * order / (2 * SIZE))
    high = table.astype(jnp.bfloat16)
    low = (table - high.astype(np.float64)).astype(jnp.bfloat16)
    return high, low


def dot(a, b):
    return lax.dot_general(a, b, (((1,), (0,)), ((), ())), preferred_element_type=F32)


def dot_nt(a, b):
    return lax.dot_general(a, b, (((1,), (1,)), ((), ())), preferred_element_type=F32)


def dot_tn(a, b):
    return lax.dot_general(a, b, (((0,), (0,)), ((), ())), preferred_element_type=F32)


def split(x):
    high = x.astype(BF16)
    return high, (x - high.astype(F32)).astype(BF16)


def iota(shape, dim):
    return lax.broadcasted_iota(jnp.int32, shape, dim)


def choice(picks, top):
    crows = picks.shape[0]
    rows = crows * top * 2
    r1 = iota((rows, crows), 0)
    owner = GROUP * (r1 // (2 * GROUP * top)) + (r1 // top) % GROUP
    spread = (iota((rows, crows), 1) == owner).astype(F32).astype(BF16)
    r2 = iota((rows, LANES), 0)
    numbers = jnp.where(iota((rows, LANES), 1) == r2 % top, dot(spread, picks), 0.0)
    number = jnp.sum(numbers, axis=1, keepdims=True).astype(jnp.int32)
    half = (iota((rows, 1), 0) // (GROUP * top)) % 2
    return number // (SIZE // 2), 2 * (number % (SIZE // 2)) + half


def onehot(order):
    rows = order.shape[0]
    return (iota((rows, SIZE), 1) == order).astype(F32).astype(BF16)


def chosen_rows(order, top, c4h, c4l):
    rows = order.shape[0]
    hot = onehot(order)
    own = (iota((rows, GROUP * SIZE), 1) // SIZE) == ((iota((rows, GROUP * SIZE), 0) // top) % GROUP)
    high = jnp.where(own, dot(hot, c4h), 0.0).astype(BF16)
    low = jnp.where(own, dot(hot, c4l), 0.0).astype(BF16)
    return high, low


def span_mask(span, width):
    rows = span.shape[0]
    return (iota((rows, width), 1) // SIZE) == span


def forward_cols(masked, csth, cstl):
    high, low = split(masked)
    return dot_nt(high, csth) + dot_nt(low, csth) + dot_nt(high, cstl)


def pack_halves(v, top):
    step = GROUP * top
    parts = []
    for g in range(v.shape[0] // (2 * step)):
        a = v[2 * g * step : (2 * g + 1) * step]
        b = v[(2 * g + 1) * step : (2 * g + 2) * step]
        parts.append(jnp.concatenate([a, b], axis=1))
    return jnp.concatenate(parts, axis=0)


def chosen_kernel(top, me_ref, picks_ref, acts_ref, g_ref, m_ref, c4h_ref, c4l_ref, csth_ref, cstl_ref,
                  after_ref, *outs):
    del after_ref
    me = me_ref[0]
    shard = m_ref.shape[0]
    width = m_ref.shape[1]
    crows = shard // SIZE
    groups = crows // GROUP
    c4h, c4l = c4h_ref[...], c4l_ref[...]
    csth, cstl = csth_ref[...], cstl_ref[...]
    gmat = g_ref[...]
    for s in range(4):
        target = me ^ s
        span, order = choice(picks_ref[s * crows : (s + 1) * crows, :], top)
        high, low = chosen_rows(order, top, c4h, c4l)
        step = 2 * GROUP * top
        parts = []
        for g in range(groups):
            start = pl.multiple_of(target * shard + g * GROUP * SIZE, GROUP * SIZE)
            block = acts_ref[:, pl.ds(start, GROUP * SIZE)]
            both = jnp.concatenate([high[g * step : (g + 1) * step], low[g * step : (g + 1) * step]], axis=0)
            t = dot_nt(both, block)
            parts.append(t[:step] + t[step:])
        th, tl = split(jnp.concatenate(parts, axis=0))
        a = dot(th, gmat) + dot(tl, gmat)
        if s == 0:
            parts = []
            for g in range(groups):
                block = m_ref[g * GROUP * SIZE : (g + 1) * GROUP * SIZE, :]
                parts.append(
                    dot(high[g * step : (g + 1) * step], block) + dot(low[g * step : (g + 1) * step], block)
                )
            a = a + 0.9 * jnp.concatenate(parts, axis=0)
        v = forward_cols(jnp.where(span_mask(span, width), a, 0.0), csth, cstl)
        outs[s][...] = pack_halves(v, top).astype(outs[s].dtype)


def base_kernel(top, me_ref, picks_ref, v_ref, m_ref, acts_ref, ao_ref, g_ref, gp_ref, c4th_ref, c4tl_ref, csth_ref,
                cstl_ref, out_ref, a0_ref, sem):
    copy = fetch(me_ref, acts_ref, 0, 0, a0_ref, sem)
    copy.start()
    shard, width = m_ref.shape
    crows = shard // SIZE
    groups = crows // GROUP
    step = GROUP * top
    span, order = choice(picks_ref[...], top)
    hot = onehot(order)
    v = v_ref[...]
    parts = []
    for g in range(groups):
        block = v[g * step : (g + 1) * step]
        parts += [block[:, :SIZE], block[:, SIZE:]]
    vh, vl = split(jnp.concatenate(parts, axis=0))
    csth, cstl = csth_ref[...], cstl_ref[...]
    x = dot(vh, csth) + dot(vl, csth) + dot(vh, cstl)
    xh, xl = split(jnp.where(span_mask(span, width), x, 0.0))
    gmat, gpmat = g_ref[...], gp_ref[...]
    copy.wait()
    rows = GROUP * SIZE
    own = (iota((rows, 2 * step), 0) // SIZE) == ((iota((rows, 2 * step), 1) // top) % GROUP)
    for g in range(groups):
        here = slice(g * 2 * step, (g + 1) * 2 * step)
        th = jnp.where(own, dot_nt(c4th_ref[...], hot[here]), 0.0).astype(BF16)
        tl = jnp.where(own, dot_nt(c4tl_ref[...], hot[here]), 0.0).astype(BF16)
        inv = dot(th, xh[here]) + dot(tl, xh[here]) + dot(th, xl[here])
        at = slice(g * rows, (g + 1) * rows)
        pair = dot_tn(a0_ref[:, at], gmat) + dot_tn(ao_ref[:, at], gpmat)
        out_ref[at, :] = 0.9 * m_ref[at, :].astype(F32) + pair - inv


def update_kernel(top, crows, pack_ref, c2th_ref, c2tl_ref, csth_ref, cstl_ref, after_ref, out_ref, xh_ref, xl_ref):
    del after_ref
    reps = pack_ref.shape[0]
    width = out_ref.shape[1]
    per = crows * top

    @pl.when(pl.program_id(0) == 0)
    def _():
        out_ref[...] = jnp.zeros_like(out_ref)

    r1 = iota((per, crows), 0)
    spread = (iota((per, crows), 1) == r1 // top).astype(F32).astype(BF16)
    pickmask = iota((per, LANES), 1) == iota((per, LANES), 0) % top
    csth, cstl = csth_ref[...], cstl_ref[...]
    zero = jnp.zeros_like(csth)
    numbers = []
    for r in range(reps):
        v = pack_ref[r, :per, :]
        picks = pack_ref[r, per : per + crows, :]
        number = jnp.sum(jnp.where(pickmask, dot(spread, picks), 0.0), axis=1, keepdims=True).astype(jnp.int32)
        numbers.append(number)
        mask = span_mask(number // (SIZE // 2), width)
        for p in range(2):
            wh = jnp.concatenate([csth, zero] if p == 0 else [zero, csth], axis=0)
            wl = jnp.concatenate([cstl, zero] if p == 0 else [zero, cstl], axis=0)
            xh, xl = split(jnp.where(mask, dot(v, wh) + dot(v, wl), 0.0))
            xh_ref[p, r] = xh
            xl_ref[p, r] = xl
    pair = 2 * top
    cols = 2 * reps * pair
    rows = 2 * SIZE
    own = (iota((rows, cols), 0) // SIZE) == ((iota((rows, cols), 1) // top) % 2)
    for g in range(crows // 2):
        at = slice(g * pair, (g + 1) * pair)
        bh = jnp.concatenate([xh_ref[p, r, at, :] for p in range(2) for r in range(reps)], axis=0)
        bl = jnp.concatenate([xl_ref[p, r, at, :] for p in range(2) for r in range(reps)], axis=0)
        order = jnp.concatenate(
            [2 * (numbers[r][at] % (SIZE // 2)) + p for p in range(2) for r in range(reps)], axis=0
        )
        hot = onehot(order)
        th = jnp.where(own, dot_nt(c2th_ref[...], hot), 0.0).astype(BF16)
        tl = jnp.where(own, dot_nt(c2tl_ref[...], hot), 0.0).astype(BF16)
        out_ref[g * rows : (g + 1) * rows, :] += dot(th, bh) + dot(tl, bh) + dot(th, bl)


def fetch(me_ref, acts_ref, s, start, cols, sem):
    shard = acts_ref.shape[1] // 4
    at = pl.multiple_of((me_ref[0] ^ s) * shard + start, LANES)
    return pltpu.make_async_copy(acts_ref.at[:, pl.ds(at, cols.shape[1])], cols, sem)


def cut_kernel(cuts, me_ref, acts_ref, after_ref, out_ref, sems):
    del after_ref
    shard = acts_ref.shape[1] // 4
    copies, to = [], 0
    for n, (s, start, size) in enumerate(cuts):
        at = pl.multiple_of((me_ref[0] ^ s) * shard + start, LANES)
        copies.append(
            pltpu.make_async_copy(acts_ref.at[:, pl.ds(at, size)], out_ref.at[:, to : to + size], sems.at[n])
        )
        to += size
    for copy in copies:
        copy.start()
    for copy in copies:
        copy.wait()


def sum_kernel(start, me_ref, acts_ref, g_ref, gp_ref, theirs_ref, after_ref, out_ref, cols, sem):
    del after_ref
    copy = fetch(me_ref, acts_ref, 2, start, cols, sem)
    copy.start()
    part = dot_tn(theirs_ref[...], gp_ref[...])
    copy.wait()
    out_ref[...] = (part + dot_tn(cols[...], g_ref[...])).astype(BF16)


def hold_kernel(x_ref, after_ref, out_ref):
    del x_ref, after_ref, out_ref


def pack_kernel(own_ref, got1_ref, got2_ref, got3_ref, picks_ref, values_ref, pack_ref):
    count = own_ref.shape[0]
    values = own_ref[...] + got1_ref[...].astype(F32) + got2_ref[...].astype(F32) + got3_ref[...].astype(F32)
    values_ref[...] = values
    pack_ref[:count, :] = values.astype(BF16)
    pack_ref[count:, :] = picks_ref[...]


VMEM = functools.partial(pl.BlockSpec, memory_space=pltpu.VMEM)
SMEM = pl.BlockSpec(memory_space=pltpu.SMEM)
ANY = pl.BlockSpec(memory_space=pl.ANY)
HBM = pl.BlockSpec(memory_space=pltpu.HBM)
COST = pl.CostEstimate(flops=1, bytes_accessed=1, transcendentals=0)
PARAMS = pltpu.CompilerParams(vmem_limit_bytes=32 * 1024 * 1024)


def swap(x, bit, axis, size):
    return lax.ppermute(x, axis, [(i, i ^ bit) for i in range(size)])


def gather_replicas(x, replicas):
    if GATHER or replicas & (replicas - 1):
        return lax.all_gather(x, "replica", axis=0, tiled=False)
    stack, bit = x[None], 1
    while bit < replicas:
        stack = jnp.concatenate([stack, swap(stack, bit, "replica", replicas)], axis=0)
        bit *= 2
    return stack


def body(replicas, fsdp, activations, output_grads, momentum, chosen_blocks):
    old = momentum[0]
    shard, width = old.shape
    tokens = activations.shape[0]
    crows = shard // SIZE
    top = chosen_blocks.shape[2]
    lead = shard // 4
    spans = width // SIZE
    high, low = table_parts()
    c4h, c4l = (np.tile(t, (1, GROUP)) for t in (high, low))
    c4th, c4tl = (np.tile(t.T, (GROUP, 1)) for t in (high, low))
    c2th, c2tl = (np.tile(t.T, (2, 1)) for t in (high, low))
    csth, cstl = (np.tile(t, (1, spans)) for t in (high, low))
    me = lax.axis_index("fsdp")

    mine = jnp.reshape(me, (1,))
    picks = jnp.pad(chosen_blocks[0].astype(BF16), ((0, 0), (0, LANES - top)))
    count = crows * top

    def swap_near(x, bit):
        return swap(x, bit, "fsdp", fsdp)

    def call(kernel, name, outs, args, specs, cols=0):
        scratch = [pltpu.VMEM((tokens, cols), BF16), pltpu.SemaphoreType.DMA] if cols else []
        return pl.pallas_call(
            kernel,
            out_shape=outs,
            in_specs=[{"s": SMEM, "a": ANY, "h": HBM, "v": VMEM()}[c] for c in specs],
            out_specs=jax.tree.map(lambda _: VMEM(), outs),
            scratch_shapes=scratch,
            compiler_params=PARAMS,
            cost_estimate=COST,
            name=name,
        )(*args)

    def cut(cuts, after):
        return pl.pallas_call(
            functools.partial(cut_kernel, cuts),
            out_shape=bf(tokens, sum(size for _, _, size in cuts)),
            in_specs=[SMEM, HBM, ANY],
            out_specs=ANY,
            scratch_shapes=[pltpu.SemaphoreType.DMA((len(cuts),))],
            compiler_params=PARAMS,
            cost_estimate=COST,
            name="cut",
        )(mine, activations, after)

    def bf(*shape):
        return jax.ShapeDtypeStruct(shape, BF16)

    def f32(*shape):
        return jax.ShapeDtypeStruct(shape, F32)

    acts, grads = activations, output_grads
    picks4 = jnp.concatenate([picks] + [swap_near(picks, s) for s in (1, 2, 3)], axis=0)
    got_grads = swap_near(grads, 1)
    cols_1 = swap_near(cut([(3, 0, lead)], picks), 1)

    def sums(start, cols, after, name):
        size = cols.shape[1]
        kernel = functools.partial(sum_kernel, start)
        return call(kernel, name, bf(size, width), (mine, acts, grads, got_grads, cols, after), "shvvva", size)

    cut_2 = cut([(3, lead, shard - lead)], picks4)
    cols_2 = swap_near(cut_2, 1)
    sum_1 = sums(0, cols_1, cut_2, "sum_1")
    got_1 = swap_near(sum_1, 2)
    own, *parts = call(
        functools.partial(chosen_kernel, top),
        "chosen",
        [f32(count, 2 * SIZE)] + [bf(count, 2 * SIZE)] * 3,
        (mine, picks4, acts, grads, old, c4h, c4l, csth, cstl, sum_1),
        "s" + "v" * 8 + "a",
    )
    got = [swap_near(x, s + 1) for s, x in enumerate(parts)]
    values, pack = call(
        pack_kernel, "pack", [f32(count, 2 * SIZE), bf(count + crows, 2 * SIZE)], (own, *got, picks), "vvvvv"
    )
    sum_2 = sums(lead, cols_2, values, "sum_2")
    sum_2 = pl.pallas_call(
        hold_kernel,
        out_shape=bf(*sum_2.shape),
        in_specs=[ANY] * 2,
        out_specs=ANY,
        input_output_aliases={0: 0},
        compiler_params=PARAMS,
        cost_estimate=COST,
        name="hold",
    )(sum_2, got_1)
    got_2 = swap_near(sum_2, 2)
    cols_own = swap_near(cut([(1, 0, shard)], sum_2), 1)
    base = call(
        functools.partial(base_kernel, top),
        "base",
        f32(shard, width),
        (mine, picks, values, old, acts, cols_own, grads, got_grads, c4th, c4tl, csth, cstl),
        "svvvhvvvvvvv",
        shard,
    )

    everyone = gather_replicas(pack, replicas)
    step = 8 if replicas % 8 == 0 else 1
    update = pl.pallas_call(
        functools.partial(update_kernel, top, crows),
        grid=(replicas // step,),
        out_shape=jax.ShapeDtypeStruct((shard, width), F32),
        in_specs=[pl.BlockSpec((step, pack.shape[0], LANES), lambda i: (i, 0, 0))] + [VMEM()] * 4 + [ANY],
        out_specs=pl.BlockSpec((shard, width), lambda i: (0, 0)),
        scratch_shapes=[pltpu.VMEM((2, step, crows * top, width), BF16)] * 2,
        compiler_params=PARAMS,
        cost_estimate=COST,
        name="update",
    )(everyone, c2th, c2tl, csth, cstl, values)
    moment_next = (base + jnp.concatenate([got_1, got_2], axis=0).astype(F32)).astype(BF16)
    return moment_next[None], update


def solution(mesh):
    return jax.shard_map(
        functools.partial(body, mesh.shape["replica"], mesh.shape["fsdp"]),
        mesh=mesh,
        in_specs=(
            P(("replica", "fsdp"), None),
            P(("replica", "fsdp"), None),
            P("replica", "fsdp", None),
            P("replica", "fsdp", None),
        ),
        out_specs=(P("replica", "fsdp", None), P("fsdp", None)),
        check_vma=False,
    )
```

```python
import functools

import jax
import jax.numpy as jnp
import numpy as np
from jax import lax
from jax.experimental import pallas as pl
from jax.experimental.pallas import tpu as pltpu
from jax.sharding import PartitionSpec as P

F32 = jnp.float32
BF16 = jnp.bfloat16
SIZE = 64
LANES = 128
GATHER = True
GROUP = 4


def table_parts():
    order = np.arange(SIZE, dtype=np.float64)[:, None]
    place = np.arange(SIZE, dtype=np.float64)[None, :]
    factor = np.where(order == 0, np.sqrt(1.0 / SIZE), np.sqrt(2.0 / SIZE))
    table = factor * np.cos(np.pi * (2 * place + 1) * order / (2 * SIZE))
    high = table.astype(jnp.bfloat16)
    low = (table - high.astype(np.float64)).astype(jnp.bfloat16)
    return high, low


def dot(a, b):
    return lax.dot_general(a, b, (((1,), (0,)), ((), ())), preferred_element_type=F32)


def dot_nt(a, b):
    return lax.dot_general(a, b, (((1,), (1,)), ((), ())), preferred_element_type=F32)


def dot_tn(a, b):
    return lax.dot_general(a, b, (((0,), (0,)), ((), ())), preferred_element_type=F32)


def split(x):
    high = x.astype(BF16)
    return high, (x - high.astype(F32)).astype(BF16)


def iota(shape, dim):
    return lax.broadcasted_iota(jnp.int32, shape, dim)


def choice(picks, top):
    crows = picks.shape[0]
    rows = crows * top * 2
    r1 = iota((rows, crows), 0)
    owner = GROUP * (r1 // (2 * GROUP * top)) + (r1 // top) % GROUP
    spread = (iota((rows, crows), 1) == owner).astype(F32).astype(BF16)
    r2 = iota((rows, LANES), 0)
    numbers = jnp.where(iota((rows, LANES), 1) == r2 % top, dot(spread, picks), 0.0)
    number = jnp.sum(numbers, axis=1, keepdims=True).astype(jnp.int32)
    half = (iota((rows, 1), 0) // (GROUP * top)) % 2
    return number // (SIZE // 2), 2 * (number % (SIZE // 2)) + half


def onehot(order):
    rows = order.shape[0]
    return (iota((rows, SIZE), 1) == order).astype(F32).astype(BF16)


def chosen_rows(order, top, c4h, c4l):
    rows = order.shape[0]
    hot = onehot(order)
    own = (iota((rows, GROUP * SIZE), 1) // SIZE) == ((iota((rows, GROUP * SIZE), 0) // top) % GROUP)
    high = jnp.where(own, dot(hot, c4h), 0.0).astype(BF16)
    low = jnp.where(own, dot(hot, c4l), 0.0).astype(BF16)
    return high, low


def span_mask(span, width):
    rows = span.shape[0]
    return (iota((rows, width), 1) // SIZE) == span


def forward_cols(masked, csth, cstl):
    high, low = split(masked)
    return dot_nt(high, csth) + dot_nt(low, csth) + dot_nt(high, cstl)


def pack_halves(v, top):
    step = GROUP * top
    parts = []
    for g in range(v.shape[0] // (2 * step)):
        a = v[2 * g * step : (2 * g + 1) * step]
        b = v[(2 * g + 1) * step : (2 * g + 2) * step]
        parts.append(jnp.concatenate([a, b], axis=1))
    return jnp.concatenate(parts, axis=0)


def chosen_kernel(top, me_ref, picks_ref, acts_ref, g_ref, m_ref, c4h_ref, c4l_ref, csth_ref, cstl_ref,
                  after_ref, *outs):
    del after_ref
    me = me_ref[0]
    shard = m_ref.shape[0]
    width = m_ref.shape[1]
    crows = shard // SIZE
    groups = crows // GROUP
    c4h, c4l = c4h_ref[...], c4l_ref[...]
    csth, cstl = csth_ref[...], cstl_ref[...]
    gmat = g_ref[...]
    for s in range(4):
        target = me ^ s
        span, order = choice(picks_ref[s * crows : (s + 1) * crows, :], top)
        high, low = chosen_rows(order, top, c4h, c4l)
        step = 2 * GROUP * top
        parts = []
        for g in range(groups):
            start = pl.multiple_of(target * shard + g * GROUP * SIZE, GROUP * SIZE)
            block = acts_ref[:, pl.ds(start, GROUP * SIZE)]
            both = jnp.concatenate([high[g * step : (g + 1) * step], low[g * step : (g + 1) * step]], axis=0)
            t = dot_nt(both, block)
            parts.append(t[:step] + t[step:])
        th, tl = split(jnp.concatenate(parts, axis=0))
        a = dot(th, gmat) + dot(tl, gmat)
        if s == 0:
            parts = []
            for g in range(groups):
                block = m_ref[g * GROUP * SIZE : (g + 1) * GROUP * SIZE, :]
                parts.append(
                    dot(high[g * step : (g + 1) * step], block) + dot(low[g * step : (g + 1) * step], block)
                )
            a = a + 0.9 * jnp.concatenate(parts, axis=0)
        v = forward_cols(jnp.where(span_mask(span, width), a, 0.0), csth, cstl)
        outs[s][...] = pack_halves(v, top).astype(outs[s].dtype)


def base_kernel(top, me_ref, picks_ref, v_ref, m_ref, acts_ref, ao_ref, g_ref, gp_ref, c4th_ref, c4tl_ref, csth_ref,
                cstl_ref, out_ref, a0_ref, sem):
    copy = fetch(me_ref, acts_ref, 0, 0, a0_ref, sem)
    copy.start()
    shard, width = m_ref.shape
    crows = shard // SIZE
    groups = crows // GROUP
    step = GROUP * top
    span, order = choice(picks_ref[...], top)
    hot = onehot(order)
    v = v_ref[...]
    parts = []
    for g in range(groups):
        block = v[g * step : (g + 1) * step]
        parts += [block[:, :SIZE], block[:, SIZE:]]
    vh, vl = split(jnp.concatenate(parts, axis=0))
    csth, cstl = csth_ref[...], cstl_ref[...]
    x = dot(vh, csth) + dot(vl, csth) + dot(vh, cstl)
    xh, xl = split(jnp.where(span_mask(span, width), x, 0.0))
    gmat, gpmat = g_ref[...], gp_ref[...]
    copy.wait()
    rows = GROUP * SIZE
    own = (iota((rows, 2 * step), 0) // SIZE) == ((iota((rows, 2 * step), 1) // top) % GROUP)
    for g in range(groups):
        here = slice(g * 2 * step, (g + 1) * 2 * step)
        th = jnp.where(own, dot_nt(c4th_ref[...], hot[here]), 0.0).astype(BF16)
        tl = jnp.where(own, dot_nt(c4tl_ref[...], hot[here]), 0.0).astype(BF16)
        inv = dot(th, xh[here]) + dot(tl, xh[here]) + dot(th, xl[here])
        at = slice(g * rows, (g + 1) * rows)
        pair = dot_tn(a0_ref[:, at], gmat) + dot_tn(ao_ref[:, at], gpmat)
        out_ref[at, :] = 0.9 * m_ref[at, :].astype(F32) + pair - inv


def update_kernel(top, crows, pack_ref, c2th_ref, c2tl_ref, csth_ref, cstl_ref, after_ref, out_ref, xh_ref, xl_ref):
    del after_ref
    reps = pack_ref.shape[0]
    width = out_ref.shape[1]
    per = crows * top

    @pl.when(pl.program_id(0) == 0)
    def _():
        out_ref[...] = jnp.zeros_like(out_ref)

    r1 = iota((per, crows), 0)
    spread = (iota((per, crows), 1) == r1 // top).astype(F32).astype(BF16)
    pickmask = iota((per, LANES), 1) == iota((per, LANES), 0) % top
    csth, cstl = csth_ref[...], cstl_ref[...]
    zero = jnp.zeros_like(csth)
    numbers = []
    for r in range(reps):
        v = pack_ref[r, :per, :]
        picks = pack_ref[r, per : per + crows, :]
        number = jnp.sum(jnp.where(pickmask, dot(spread, picks), 0.0), axis=1, keepdims=True).astype(jnp.int32)
        numbers.append(number)
        mask = span_mask(number // (SIZE // 2), width)
        for p in range(2):
            wh = jnp.concatenate([csth, zero] if p == 0 else [zero, csth], axis=0)
            wl = jnp.concatenate([cstl, zero] if p == 0 else [zero, cstl], axis=0)
            xh, xl = split(jnp.where(mask, dot(v, wh) + dot(v, wl), 0.0))
            xh_ref[p, r] = xh
            xl_ref[p, r] = xl
    pair = 2 * top
    cols = 2 * reps * pair
    rows = 2 * SIZE
    own = (iota((rows, cols), 0) // SIZE) == ((iota((rows, cols), 1) // top) % 2)
    for g in range(crows // 2):
        at = slice(g * pair, (g + 1) * pair)
        bh = jnp.concatenate([xh_ref[p, r, at, :] for p in range(2) for r in range(reps)], axis=0)
        bl = jnp.concatenate([xl_ref[p, r, at, :] for p in range(2) for r in range(reps)], axis=0)
        order = jnp.concatenate(
            [2 * (numbers[r][at] % (SIZE // 2)) + p for p in range(2) for r in range(reps)], axis=0
        )
        hot = onehot(order)
        th = jnp.where(own, dot_nt(c2th_ref[...], hot), 0.0).astype(BF16)
        tl = jnp.where(own, dot_nt(c2tl_ref[...], hot), 0.0).astype(BF16)
        out_ref[g * rows : (g + 1) * rows, :] += dot(th, bh) + dot(tl, bh) + dot(th, bl)


def fetch(me_ref, acts_ref, s, start, cols, sem):
    shard = acts_ref.shape[1] // 4
    at = pl.multiple_of((me_ref[0] ^ s) * shard + start, LANES)
    return pltpu.make_async_copy(acts_ref.at[:, pl.ds(at, cols.shape[1])], cols, sem)


def cut_kernel(cuts, me_ref, acts_ref, after_ref, after2_ref, after3_ref, out_ref, sems):
    del after_ref, after2_ref, after3_ref
    shard = acts_ref.shape[1] // 4
    copies, to = [], 0
    for n, (s, start, size) in enumerate(cuts):
        at = pl.multiple_of((me_ref[0] ^ s) * shard + start, LANES)
        copies.append(
            pltpu.make_async_copy(acts_ref.at[:, pl.ds(at, size)], out_ref.at[:, to : to + size], sems.at[n])
        )
        to += size
    for copy in copies:
        copy.start()
    for copy in copies:
        copy.wait()


def sum_kernel(start, me_ref, acts_ref, g_ref, gp_ref, theirs_ref, after_ref, out_ref, cols, sem):
    del after_ref
    copy = fetch(me_ref, acts_ref, 2, start, cols, sem)
    copy.start()
    part = dot_tn(theirs_ref[...], gp_ref[...])
    copy.wait()
    out_ref[...] = (part + dot_tn(cols[...], g_ref[...])).astype(BF16)


def hold_kernel(x_ref, after_ref, after2_ref, out_ref):
    del x_ref, after_ref, after2_ref, out_ref


def final_kernel(base_ref, got1_ref, got2_ref, out_ref, rows, sems):
    size = rows.shape[1]
    copies = []
    for n in range(rows.shape[0]):
        got = got1_ref[...] if n == 0 else got2_ref[(n - 1) * size : n * size, :]
        rows[n] = (base_ref[n * size : (n + 1) * size, :] + got.astype(F32)).astype(BF16)
        copies.append(pltpu.make_async_copy(rows.at[n], out_ref.at[n * size : (n + 1) * size], sems.at[n]))
        copies[-1].start()
    for copy in copies:
        copy.wait()


def pack_kernel(own_ref, got1_ref, got2_ref, got3_ref, picks_ref, after_ref, values_ref, pack_ref):
    del after_ref
    count = own_ref.shape[0]
    values = own_ref[...] + got1_ref[...].astype(F32) + got2_ref[...].astype(F32) + got3_ref[...].astype(F32)
    values_ref[...] = values
    pack_ref[:count, :] = values.astype(BF16)
    pack_ref[count:, :] = picks_ref[...]


VMEM = functools.partial(pl.BlockSpec, memory_space=pltpu.VMEM)
SMEM = pl.BlockSpec(memory_space=pltpu.SMEM)
ANY = pl.BlockSpec(memory_space=pl.ANY)
HBM = pl.BlockSpec(memory_space=pltpu.HBM)
COST = pl.CostEstimate(flops=1, bytes_accessed=1, transcendentals=0)
PARAMS = pltpu.CompilerParams(vmem_limit_bytes=32 * 1024 * 1024)


def swap(x, bit, axis, size):
    return lax.ppermute(x, axis, [(i, i ^ bit) for i in range(size)])


def gather_replicas(x, replicas):
    if GATHER or replicas & (replicas - 1):
        return lax.all_gather(x, "replica", axis=0, tiled=False)
    stack, bit = x[None], 1
    while bit < replicas:
        stack = jnp.concatenate([stack, swap(stack, bit, "replica", replicas)], axis=0)
        bit *= 2
    return stack


def body(replicas, fsdp, activations, output_grads, momentum, chosen_blocks):
    old = momentum[0]
    shard, width = old.shape
    tokens = activations.shape[0]
    crows = shard // SIZE
    top = chosen_blocks.shape[2]
    lead = shard // 4
    spans = width // SIZE
    high, low = table_parts()
    c4h, c4l = (np.tile(t, (1, GROUP)) for t in (high, low))
    c4th, c4tl = (np.tile(t.T, (GROUP, 1)) for t in (high, low))
    c2th, c2tl = (np.tile(t.T, (2, 1)) for t in (high, low))
    csth, cstl = (np.tile(t, (1, spans)) for t in (high, low))
    me = lax.axis_index("fsdp")

    mine = jnp.reshape(me, (1,))
    picks = jnp.pad(chosen_blocks[0].astype(BF16), ((0, 0), (0, LANES - top)))
    count = crows * top

    def swap_near(x, bit):
        return swap(x, bit, "fsdp", fsdp)

    def call(kernel, name, outs, args, specs, cols=0):
        scratch = [pltpu.VMEM((tokens, cols), BF16), pltpu.SemaphoreType.DMA] if cols else []
        return pl.pallas_call(
            kernel,
            out_shape=outs,
            in_specs=[{"s": SMEM, "a": ANY, "h": HBM, "v": VMEM()}[c] for c in specs],
            out_specs=jax.tree.map(lambda _: VMEM(), outs),
            scratch_shapes=scratch,
            compiler_params=PARAMS,
            cost_estimate=COST,
            name=name,
        )(*args)

    def cut(cuts, after, after2, after3):
        return pl.pallas_call(
            functools.partial(cut_kernel, cuts),
            out_shape=bf(tokens, sum(size for _, _, size in cuts)),
            in_specs=[SMEM, HBM, ANY, ANY, ANY],
            out_specs=ANY,
            scratch_shapes=[pltpu.SemaphoreType.DMA((len(cuts),))],
            compiler_params=PARAMS,
            cost_estimate=COST,
            name="cut",
        )(mine, activations, after, after2, after3)

    def bf(*shape):
        return jax.ShapeDtypeStruct(shape, BF16)

    def f32(*shape):
        return jax.ShapeDtypeStruct(shape, F32)

    acts, grads = activations, output_grads
    picks4 = jnp.concatenate([picks] + [swap_near(picks, s) for s in (1, 2, 3)], axis=0)
    got_grads = swap_near(grads, 1)
    cols_1 = swap_near(cut([(3, 0, lead)], picks, picks, picks), 1)

    def sums(start, cols, after, name):
        size = cols.shape[1]
        kernel = functools.partial(sum_kernel, start)
        return call(kernel, name, bf(size, width), (mine, acts, grads, got_grads, cols, after), "shvvva", size)

    cut_2 = cut([(3, lead, shard - lead)], picks4, cols_1, got_grads)
    cols_2 = swap_near(cut_2, 1)
    sum_1 = sums(0, cols_1, cols_1, "sum_1")
    got_1 = swap_near(sum_1, 2)
    own, *parts = call(
        functools.partial(chosen_kernel, top),
        "chosen",
        [f32(count, 2 * SIZE)] + [bf(count, 2 * SIZE)] * 3,
        (mine, picks4, acts, grads, old, c4h, c4l, csth, cstl, sum_1),
        "s" + "v" * 8 + "a",
    )
    got = [swap_near(x, s + 1) for s, x in enumerate(parts)]
    sum_2 = sums(lead, cols_2, parts[0], "sum_2")
    values, pack = call(
        pack_kernel, "pack", [f32(count, 2 * SIZE), bf(count + crows, 2 * SIZE)], (own, *got, picks, sum_2), "vvvvva"
    )
    sum_2 = pl.pallas_call(
        hold_kernel,
        out_shape=bf(*sum_2.shape),
        in_specs=[ANY] * 3,
        out_specs=ANY,
        input_output_aliases={0: 0},
        compiler_params=PARAMS,
        cost_estimate=COST,
        name="hold",
    )(sum_2, got_1, values)
    got_2 = swap_near(sum_2, 2)
    cols_own = swap_near(cut([(1, 0, shard)], sum_2, sum_2, sum_2), 1)
    base = call(
        functools.partial(base_kernel, top),
        "base",
        f32(shard, width),
        (mine, picks, values, old, acts, cols_own, grads, got_grads, c4th, c4tl, csth, cstl),
        "svvvhvvvvvvv",
        shard,
    )

    everyone = gather_replicas(pack, replicas)
    step = 8 if replicas % 8 == 0 else 1
    update = pl.pallas_call(
        functools.partial(update_kernel, top, crows),
        grid=(replicas // step,),
        out_shape=jax.ShapeDtypeStruct((shard, width), F32),
        in_specs=[pl.BlockSpec((step, pack.shape[0], LANES), lambda i: (i, 0, 0))] + [VMEM()] * 4 + [ANY],
        out_specs=pl.BlockSpec((shard, width), lambda i: (0, 0)),
        scratch_shapes=[pltpu.VMEM((2, step, crows * top, width), BF16)] * 2,
        compiler_params=PARAMS,
        cost_estimate=COST,
        name="update",
    )(everyone, c2th, c2tl, csth, cstl, values)
    moment_next = pl.pallas_call(
        final_kernel,
        out_shape=bf(shard, width),
        in_specs=[VMEM()] * 3,
        out_specs=HBM,
        scratch_shapes=[pltpu.VMEM((shard // lead, lead, width), BF16), pltpu.SemaphoreType.DMA((shard // lead,))],
        compiler_params=PARAMS,
        cost_estimate=COST,
        name="final",
    )(base, got_1, got_2)
    return moment_next[None], update


def solution(mesh):
    return jax.shard_map(
        functools.partial(body, mesh.shape["replica"], mesh.shape["fsdp"]),
        mesh=mesh,
        in_specs=(
            P(("replica", "fsdp"), None),
            P(("replica", "fsdp"), None),
            P("replica", "fsdp", None),
            P("replica", "fsdp", None),
        ),
        out_specs=(P("replica", "fsdp", None), P("fsdp", None)),
        check_vma=False,
    )
```

```python
import functools

import jax
import jax.numpy as jnp
import numpy as np
from jax import lax
from jax.experimental import pallas as pl
from jax.experimental.pallas import tpu as pltpu
from jax.sharding import PartitionSpec as P

F32 = jnp.float32
BF16 = jnp.bfloat16
SIZE = 64
LANES = 128
GATHER = True
SECOND = 384
GROUP = 4


def table_parts():
    order = np.arange(SIZE, dtype=np.float64)[:, None]
    place = np.arange(SIZE, dtype=np.float64)[None, :]
    factor = np.where(order == 0, np.sqrt(1.0 / SIZE), np.sqrt(2.0 / SIZE))
    table = factor * np.cos(np.pi * (2 * place + 1) * order / (2 * SIZE))
    high = table.astype(jnp.bfloat16)
    low = (table - high.astype(np.float64)).astype(jnp.bfloat16)
    return high, low


def dot(a, b):
    return lax.dot_general(a, b, (((1,), (0,)), ((), ())), preferred_element_type=F32)


def dot_nt(a, b):
    return lax.dot_general(a, b, (((1,), (1,)), ((), ())), preferred_element_type=F32)


def dot_tn(a, b):
    return lax.dot_general(a, b, (((0,), (0,)), ((), ())), preferred_element_type=F32)


def split(x):
    high = x.astype(BF16)
    return high, (x - high.astype(F32)).astype(BF16)


def iota(shape, dim):
    return lax.broadcasted_iota(jnp.int32, shape, dim)


def choice(picks, top):
    crows = picks.shape[0]
    rows = crows * top * 2
    r1 = iota((rows, crows), 0)
    owner = GROUP * (r1 // (2 * GROUP * top)) + (r1 // top) % GROUP
    spread = (iota((rows, crows), 1) == owner).astype(F32).astype(BF16)
    r2 = iota((rows, LANES), 0)
    numbers = jnp.where(iota((rows, LANES), 1) == r2 % top, dot(spread, picks), 0.0)
    number = jnp.sum(numbers, axis=1, keepdims=True).astype(jnp.int32)
    half = (iota((rows, 1), 0) // (GROUP * top)) % 2
    return number // (SIZE // 2), 2 * (number % (SIZE // 2)) + half


def onehot(order):
    rows = order.shape[0]
    return (iota((rows, SIZE), 1) == order).astype(F32).astype(BF16)


def chosen_rows(order, top, c4h, c4l):
    rows = order.shape[0]
    hot = onehot(order)
    own = (iota((rows, GROUP * SIZE), 1) // SIZE) == ((iota((rows, GROUP * SIZE), 0) // top) % GROUP)
    high = jnp.where(own, dot(hot, c4h), 0.0).astype(BF16)
    low = jnp.where(own, dot(hot, c4l), 0.0).astype(BF16)
    return high, low


def span_mask(span, width):
    rows = span.shape[0]
    return (iota((rows, width), 1) // SIZE) == span


def forward_cols(masked, csth, cstl):
    high, low = split(masked)
    return dot_nt(high, csth) + dot_nt(low, csth) + dot_nt(high, cstl)


def pack_halves(v, top):
    step = GROUP * top
    parts = []
    for g in range(v.shape[0] // (2 * step)):
        a = v[2 * g * step : (2 * g + 1) * step]
        b = v[(2 * g + 1) * step : (2 * g + 2) * step]
        parts.append(jnp.concatenate([a, b], axis=1))
    return jnp.concatenate(parts, axis=0)


def chosen_kernel(top, me_ref, picks_ref, acts_ref, g_ref, m_ref, c4h_ref, c4l_ref, csth_ref, cstl_ref,
                  after_ref, *outs):
    del after_ref
    me = me_ref[0]
    shard = m_ref.shape[0]
    width = m_ref.shape[1]
    crows = shard // SIZE
    groups = crows // GROUP
    c4h, c4l = c4h_ref[...], c4l_ref[...]
    csth, cstl = csth_ref[...], cstl_ref[...]
    gmat = g_ref[...]
    for s in range(4):
        target = me ^ s
        span, order = choice(picks_ref[s * crows : (s + 1) * crows, :], top)
        high, low = chosen_rows(order, top, c4h, c4l)
        step = 2 * GROUP * top
        parts = []
        for g in range(groups):
            start = pl.multiple_of(target * shard + g * GROUP * SIZE, GROUP * SIZE)
            block = acts_ref[:, pl.ds(start, GROUP * SIZE)]
            both = jnp.concatenate([high[g * step : (g + 1) * step], low[g * step : (g + 1) * step]], axis=0)
            t = dot_nt(both, block)
            parts.append(t[:step] + t[step:])
        th, tl = split(jnp.concatenate(parts, axis=0))
        a = dot(th, gmat) + dot(tl, gmat)
        if s == 0:
            parts = []
            for g in range(groups):
                block = m_ref[g * GROUP * SIZE : (g + 1) * GROUP * SIZE, :]
                parts.append(
                    dot(high[g * step : (g + 1) * step], block) + dot(low[g * step : (g + 1) * step], block)
                )
            a = a + 0.9 * jnp.concatenate(parts, axis=0)
        v = forward_cols(jnp.where(span_mask(span, width), a, 0.0), csth, cstl)
        outs[s][...] = pack_halves(v, top).astype(outs[s].dtype)


def base_kernel(top, me_ref, picks_ref, v_ref, m_ref, acts_ref, ao1_ref, ao2_ref, g_ref, gp_ref, c4th_ref, c4tl_ref, csth_ref,
                cstl_ref, out_ref, a0_ref, sem):
    copy = fetch(me_ref, acts_ref, 0, 0, a0_ref, sem)
    copy.start()
    shard, width = m_ref.shape
    crows = shard // SIZE
    groups = crows // GROUP
    step = GROUP * top
    span, order = choice(picks_ref[...], top)
    hot = onehot(order)
    v = v_ref[...]
    parts = []
    for g in range(groups):
        block = v[g * step : (g + 1) * step]
        parts += [block[:, :SIZE], block[:, SIZE:]]
    vh, vl = split(jnp.concatenate(parts, axis=0))
    csth, cstl = csth_ref[...], cstl_ref[...]
    x = dot(vh, csth) + dot(vl, csth) + dot(vh, cstl)
    xh, xl = split(jnp.where(span_mask(span, width), x, 0.0))
    gmat, gpmat = g_ref[...], gp_ref[...]
    copy.wait()
    rows = GROUP * SIZE
    own = (iota((rows, 2 * step), 0) // SIZE) == ((iota((rows, 2 * step), 1) // top) % GROUP)
    for g in range(groups):
        here = slice(g * 2 * step, (g + 1) * 2 * step)
        th = jnp.where(own, dot_nt(c4th_ref[...], hot[here]), 0.0).astype(BF16)
        tl = jnp.where(own, dot_nt(c4tl_ref[...], hot[here]), 0.0).astype(BF16)
        inv = dot(th, xh[here]) + dot(tl, xh[here]) + dot(th, xl[here])
        at = slice(g * rows, (g + 1) * rows)
        ao_ref, first = (ao1_ref, 0) if 2 * g < groups else (ao2_ref, shard // 2)
        theirs = ao_ref[:, g * rows - first : (g + 1) * rows - first]
        pair = dot_tn(a0_ref[:, at], gmat) + dot_tn(theirs, gpmat)
        out_ref[at, :] = 0.9 * m_ref[at, :].astype(F32) + pair - inv


def update_kernel(top, crows, pack_ref, c2th_ref, c2tl_ref, csth_ref, cstl_ref, after_ref, out_ref, xh_ref, xl_ref):
    del after_ref
    reps = pack_ref.shape[0]
    width = out_ref.shape[1]
    per = crows * top

    @pl.when(pl.program_id(0) == 0)
    def _():
        out_ref[...] = jnp.zeros_like(out_ref)

    r1 = iota((per, crows), 0)
    spread = (iota((per, crows), 1) == r1 // top).astype(F32).astype(BF16)
    pickmask = iota((per, LANES), 1) == iota((per, LANES), 0) % top
    csth, cstl = csth_ref[...], cstl_ref[...]
    zero = jnp.zeros_like(csth)
    numbers = []
    for r in range(reps):
        v = pack_ref[r, :per, :]
        picks = pack_ref[r, per : per + crows, :]
        number = jnp.sum(jnp.where(pickmask, dot(spread, picks), 0.0), axis=1, keepdims=True).astype(jnp.int32)
        numbers.append(number)
        mask = span_mask(number // (SIZE // 2), width)
        for p in range(2):
            wh = jnp.concatenate([csth, zero] if p == 0 else [zero, csth], axis=0)
            wl = jnp.concatenate([cstl, zero] if p == 0 else [zero, cstl], axis=0)
            xh, xl = split(jnp.where(mask, dot(v, wh) + dot(v, wl), 0.0))
            xh_ref[p, r] = xh
            xl_ref[p, r] = xl
    pair = 2 * top
    cols = 2 * reps * pair
    rows = 2 * SIZE
    own = (iota((rows, cols), 0) // SIZE) == ((iota((rows, cols), 1) // top) % 2)
    for g in range(crows // 2):
        at = slice(g * pair, (g + 1) * pair)
        bh = jnp.concatenate([xh_ref[p, r, at, :] for p in range(2) for r in range(reps)], axis=0)
        bl = jnp.concatenate([xl_ref[p, r, at, :] for p in range(2) for r in range(reps)], axis=0)
        order = jnp.concatenate(
            [2 * (numbers[r][at] % (SIZE // 2)) + p for p in range(2) for r in range(reps)], axis=0
        )
        hot = onehot(order)
        th = jnp.where(own, dot_nt(c2th_ref[...], hot), 0.0).astype(BF16)
        tl = jnp.where(own, dot_nt(c2tl_ref[...], hot), 0.0).astype(BF16)
        out_ref[g * rows : (g + 1) * rows, :] += dot(th, bh) + dot(tl, bh) + dot(th, bl)


def fetch(me_ref, acts_ref, s, start, cols, sem):
    shard = acts_ref.shape[1] // 4
    at = pl.multiple_of((me_ref[0] ^ s) * shard + start, LANES)
    return pltpu.make_async_copy(acts_ref.at[:, pl.ds(at, cols.shape[1])], cols, sem)


def cut_kernel(cuts, me_ref, acts_ref, after_ref, after2_ref, after3_ref, out_ref, sems):
    del after_ref, after2_ref, after3_ref
    shard = acts_ref.shape[1] // 4
    copies, to = [], 0
    for n, (s, start, size) in enumerate(cuts):
        at = pl.multiple_of((me_ref[0] ^ s) * shard + start, LANES)
        copies.append(
            pltpu.make_async_copy(acts_ref.at[:, pl.ds(at, size)], out_ref.at[:, to : to + size], sems.at[n])
        )
        to += size
    for copy in copies:
        copy.start()
    for copy in copies:
        copy.wait()


def sum_kernel(start, me_ref, acts_ref, g_ref, gp_ref, theirs_ref, after_ref, out_ref, cols, sem):
    del after_ref
    copy = fetch(me_ref, acts_ref, 2, start, cols, sem)
    copy.start()
    part = dot_tn(theirs_ref[...], gp_ref[...])
    copy.wait()
    out_ref[...] = (part + dot_tn(cols[...], g_ref[...])).astype(BF16)


def hold_kernel(x_ref, after_ref, after2_ref, out_ref):
    del x_ref, after_ref, after2_ref, out_ref


def early_kernel(base_ref, got1_ref, got2_ref, out_ref, rows, sems):
    copies, at = [], 0
    for n, got_ref in enumerate((got1_ref, got2_ref)):
        here = slice(at, at + got_ref.shape[0])
        rows[here, :] = (base_ref[here, :] + got_ref[...].astype(F32)).astype(BF16)
        copies.append(pltpu.make_async_copy(rows.at[here], out_ref.at[here], sems.at[n]))
        copies[-1].start()
        at += got_ref.shape[0]
    for copy in copies:
        copy.wait()


def last_kernel(base_ref, got_ref, early_ref, out_ref, rows, sems):
    del early_ref
    shard = base_ref.shape[0]
    size = got_ref.shape[0] // 2
    copies = []
    for n in range(2):
        here = slice(n * size, (n + 1) * size)
        there = slice(shard - (2 - n) * size, shard - (1 - n) * size)
        rows[here, :] = (base_ref[there, :] + got_ref[here, :].astype(F32)).astype(BF16)
        copies.append(pltpu.make_async_copy(rows.at[here], out_ref.at[there], sems.at[n]))
        copies[-1].start()
    for copy in copies:
        copy.wait()


def pack_kernel(own_ref, got1_ref, got2_ref, got3_ref, picks_ref, after_ref, values_ref, pack_ref):
    del after_ref
    count = own_ref.shape[0]
    values = own_ref[...] + got1_ref[...].astype(F32) + got2_ref[...].astype(F32) + got3_ref[...].astype(F32)
    values_ref[...] = values
    pack_ref[:count, :] = values.astype(BF16)
    pack_ref[count:, :] = picks_ref[...]


VMEM = functools.partial(pl.BlockSpec, memory_space=pltpu.VMEM)
SMEM = pl.BlockSpec(memory_space=pltpu.SMEM)
ANY = pl.BlockSpec(memory_space=pl.ANY)
HBM = pl.BlockSpec(memory_space=pltpu.HBM)
COST = pl.CostEstimate(flops=1, bytes_accessed=1, transcendentals=0)
PARAMS = pltpu.CompilerParams(vmem_limit_bytes=32 * 1024 * 1024)


def swap(x, bit, axis, size):
    return lax.ppermute(x, axis, [(i, i ^ bit) for i in range(size)])


def gather_replicas(x, replicas):
    if GATHER or replicas & (replicas - 1):
        return lax.all_gather(x, "replica", axis=0, tiled=False)
    stack, bit = x[None], 1
    while bit < replicas:
        stack = jnp.concatenate([stack, swap(stack, bit, "replica", replicas)], axis=0)
        bit *= 2
    return stack


def body(replicas, fsdp, activations, output_grads, momentum, chosen_blocks):
    old = momentum[0]
    shard, width = old.shape
    tokens = activations.shape[0]
    crows = shard // SIZE
    top = chosen_blocks.shape[2]
    lead = shard // 4
    second = SECOND
    spans = width // SIZE
    high, low = table_parts()
    c4h, c4l = (np.tile(t, (1, GROUP)) for t in (high, low))
    c4th, c4tl = (np.tile(t.T, (GROUP, 1)) for t in (high, low))
    c2th, c2tl = (np.tile(t.T, (2, 1)) for t in (high, low))
    csth, cstl = (np.tile(t, (1, spans)) for t in (high, low))
    me = lax.axis_index("fsdp")

    mine = jnp.reshape(me, (1,))
    picks = jnp.pad(chosen_blocks[0].astype(BF16), ((0, 0), (0, LANES - top)))
    count = crows * top

    def swap_near(x, bit):
        return swap(x, bit, "fsdp", fsdp)

    def call(kernel, name, outs, args, specs, cols=0):
        scratch = [pltpu.VMEM((tokens, cols), BF16), pltpu.SemaphoreType.DMA] if cols else []
        return pl.pallas_call(
            kernel,
            out_shape=outs,
            in_specs=[{"s": SMEM, "a": ANY, "h": HBM, "v": VMEM()}[c] for c in specs],
            out_specs=jax.tree.map(lambda _: VMEM(), outs),
            scratch_shapes=scratch,
            compiler_params=PARAMS,
            cost_estimate=COST,
            name=name,
        )(*args)

    def cut(cuts, after, after2, after3):
        return pl.pallas_call(
            functools.partial(cut_kernel, cuts),
            out_shape=bf(tokens, sum(size for _, _, size in cuts)),
            in_specs=[SMEM, HBM, ANY, ANY, ANY],
            out_specs=ANY,
            scratch_shapes=[pltpu.SemaphoreType.DMA((len(cuts),))],
            compiler_params=PARAMS,
            cost_estimate=COST,
            name="cut",
        )(mine, activations, after, after2, after3)

    def bf(*shape):
        return jax.ShapeDtypeStruct(shape, BF16)

    def f32(*shape):
        return jax.ShapeDtypeStruct(shape, F32)

    acts, grads = activations, output_grads
    got_picks = [swap_near(picks, s) for s in (1, 2, 3)]
    got_grads = swap_near(grads, 1)
    cols_1 = swap_near(cut([(3, 0, lead)], picks, picks, picks), 1)

    def sums(start, cols, after, name):
        size = cols.shape[1]
        kernel = functools.partial(sum_kernel, start)
        return call(kernel, name, bf(size, width), (mine, acts, grads, got_grads, cols, after), "shvvva", size)

    sum_1 = sums(0, cols_1, cols_1, "sum_1")
    got_1 = swap_near(sum_1, 2)
    picks4 = jnp.concatenate([picks, *got_picks], axis=0)
    cut_2 = cut([(3, lead, second)], picks4, cols_1, got_grads)
    cols_2 = swap_near(cut_2, 1)
    own, *parts = call(
        functools.partial(chosen_kernel, top),
        "chosen",
        [f32(count, 2 * SIZE)] + [bf(count, 2 * SIZE)] * 3,
        (mine, picks4, acts, grads, old, c4h, c4l, csth, cstl, sum_1),
        "s" + "v" * 8 + "a",
    )
    got = [swap_near(x, s + 1) for s, x in enumerate(parts)]
    sum_2 = sums(lead, cols_2, got_1, "sum_2")
    values, pack = call(
        pack_kernel, "pack", [f32(count, 2 * SIZE), bf(count + crows, 2 * SIZE)], (own, *got, picks, sum_2), "vvvvva"
    )
    sum_2 = pl.pallas_call(
        hold_kernel,
        out_shape=bf(*sum_2.shape),
        in_specs=[ANY] * 3,
        out_specs=ANY,
        input_output_aliases={0: 0},
        compiler_params=PARAMS,
        cost_estimate=COST,
        name="hold",
    )(sum_2, got_1, values)
    got_2 = swap_near(sum_2, 2)
    cols_3 = swap_near(cut([(3, lead + second, shard - lead - second)], values, values, values), 1)
    sum_3 = sums(lead + second, cols_3, sum_2, "sum_3")
    got_3 = swap_near(sum_3, 2)
    cols_own = [
        swap_near(cut([(1, n * (shard // 2), shard // 2)], sum_3, sum_3, sum_3), 1) for n in range(2)
    ]
    base = call(
        functools.partial(base_kernel, top),
        "base",
        f32(shard, width),
        (mine, picks, values, old, acts, *cols_own, grads, got_grads, c4th, c4tl, csth, cstl),
        "svvvhvvvvvvvv",
        shard,
    )

    everyone = gather_replicas(pack, replicas)
    step = 8 if replicas % 8 == 0 else 1
    update = pl.pallas_call(
        functools.partial(update_kernel, top, crows),
        grid=(replicas // step,),
        out_shape=jax.ShapeDtypeStruct((shard, width), F32),
        in_specs=[pl.BlockSpec((step, pack.shape[0], LANES), lambda i: (i, 0, 0))] + [VMEM()] * 4 + [ANY],
        out_specs=pl.BlockSpec((shard, width), lambda i: (0, 0)),
        scratch_shapes=[pltpu.VMEM((2, step, crows * top, width), BF16)] * 2,
        compiler_params=PARAMS,
        cost_estimate=COST,
        name="update",
    )(everyone, c2th, c2tl, csth, cstl, values)
    early = pl.pallas_call(
        early_kernel,
        out_shape=bf(shard, width),
        in_specs=[VMEM()] * 3,
        out_specs=HBM,
        scratch_shapes=[pltpu.VMEM((lead + second, width), BF16), pltpu.SemaphoreType.DMA((2,))],
        compiler_params=PARAMS,
        cost_estimate=COST,
        name="early",
    )(base, got_1, got_2)
    moment_next = pl.pallas_call(
        last_kernel,
        out_shape=bf(shard, width),
        in_specs=[VMEM(), VMEM(), HBM],
        out_specs=HBM,
        scratch_shapes=[pltpu.VMEM((shard - lead - second, width), BF16), pltpu.SemaphoreType.DMA((2,))],
        input_output_aliases={2: 0},
        compiler_params=PARAMS,
        cost_estimate=COST,
        name="last",
    )(base, got_3, early)
    return moment_next[None], update


def solution(mesh):
    return jax.shard_map(
        functools.partial(body, mesh.shape["replica"], mesh.shape["fsdp"]),
        mesh=mesh,
        in_specs=(
            P(("replica", "fsdp"), None),
            P(("replica", "fsdp"), None),
            P("replica", "fsdp", None),
            P("replica", "fsdp", None),
        ),
        out_specs=(P("replica", "fsdp", None), P("fsdp", None)),
        check_vma=False,
    )
```

```python
import functools

import jax
import jax.numpy as jnp
import numpy as np
from jax import lax
from jax.experimental import pallas as pl
from jax.experimental.pallas import tpu as pltpu
from jax.sharding import PartitionSpec as P

F32 = jnp.float32
BF16 = jnp.bfloat16
SIZE = 64
LANES = 128
GATHER = True
SECOND = 384
GROUP = 4


def table_parts():
    order = np.arange(SIZE, dtype=np.float64)[:, None]
    place = np.arange(SIZE, dtype=np.float64)[None, :]
    factor = np.where(order == 0, np.sqrt(1.0 / SIZE), np.sqrt(2.0 / SIZE))
    table = factor * np.cos(np.pi * (2 * place + 1) * order / (2 * SIZE))
    high = table.astype(jnp.bfloat16)
    low = (table - high.astype(np.float64)).astype(jnp.bfloat16)
    return high, low


def dot(a, b):
    return lax.dot_general(a, b, (((1,), (0,)), ((), ())), preferred_element_type=F32)


def dot_nt(a, b):
    return lax.dot_general(a, b, (((1,), (1,)), ((), ())), preferred_element_type=F32)


def dot_tn(a, b):
    return lax.dot_general(a, b, (((0,), (0,)), ((), ())), preferred_element_type=F32)


def split(x):
    high = x.astype(BF16)
    return high, (x - high.astype(F32)).astype(BF16)


def iota(shape, dim):
    return lax.broadcasted_iota(jnp.int32, shape, dim)


def choice(picks, top):
    crows = picks.shape[0]
    rows = crows * top * 2
    r1 = iota((rows, crows), 0)
    owner = GROUP * (r1 // (2 * GROUP * top)) + (r1 // top) % GROUP
    spread = (iota((rows, crows), 1) == owner).astype(F32).astype(BF16)
    r2 = iota((rows, LANES), 0)
    numbers = jnp.where(iota((rows, LANES), 1) == r2 % top, dot(spread, picks), 0.0)
    number = jnp.sum(numbers, axis=1, keepdims=True).astype(jnp.int32)
    half = (iota((rows, 1), 0) // (GROUP * top)) % 2
    return number // (SIZE // 2), 2 * (number % (SIZE // 2)) + half


def onehot(order):
    rows = order.shape[0]
    return (iota((rows, SIZE), 1) == order).astype(F32).astype(BF16)


def chosen_rows(order, top, c4h, c4l):
    rows = order.shape[0]
    hot = onehot(order)
    own = (iota((rows, GROUP * SIZE), 1) // SIZE) == ((iota((rows, GROUP * SIZE), 0) // top) % GROUP)
    high = jnp.where(own, dot(hot, c4h), 0.0).astype(BF16)
    low = jnp.where(own, dot(hot, c4l), 0.0).astype(BF16)
    return high, low


def span_mask(span, width):
    rows = span.shape[0]
    return (iota((rows, width), 1) // SIZE) == span


def forward_cols(masked, csth, cstl):
    high, low = split(masked)
    return dot_nt(high, csth) + dot_nt(low, csth) + dot_nt(high, cstl)


def pack_halves(v, top):
    step = GROUP * top
    parts = []
    for g in range(v.shape[0] // (2 * step)):
        a = v[2 * g * step : (2 * g + 1) * step]
        b = v[(2 * g + 1) * step : (2 * g + 2) * step]
        parts.append(jnp.concatenate([a, b], axis=1))
    return jnp.concatenate(parts, axis=0)


def chosen_kernel(top, me_ref, picks_ref, acts_ref, g_ref, m_ref, c4h_ref, c4l_ref, csth_ref, cstl_ref,
                  after_ref, *outs):
    del after_ref
    me = me_ref[0]
    shard = m_ref.shape[0]
    width = m_ref.shape[1]
    crows = shard // SIZE
    groups = crows // GROUP
    c4h, c4l = c4h_ref[...], c4l_ref[...]
    csth, cstl = csth_ref[...], cstl_ref[...]
    gmat = g_ref[...]
    for s in range(4):
        target = me ^ s
        span, order = choice(picks_ref[s * crows : (s + 1) * crows, :], top)
        high, low = chosen_rows(order, top, c4h, c4l)
        step = 2 * GROUP * top
        parts = []
        for g in range(groups):
            start = pl.multiple_of(target * shard + g * GROUP * SIZE, GROUP * SIZE)
            block = acts_ref[:, pl.ds(start, GROUP * SIZE)]
            both = jnp.concatenate([high[g * step : (g + 1) * step], low[g * step : (g + 1) * step]], axis=0)
            t = dot_nt(both, block)
            parts.append(t[:step] + t[step:])
        th, tl = split(jnp.concatenate(parts, axis=0))
        a = dot(th, gmat) + dot(tl, gmat)
        if s == 0:
            parts = []
            for g in range(groups):
                block = m_ref[g * GROUP * SIZE : (g + 1) * GROUP * SIZE, :]
                parts.append(
                    dot(high[g * step : (g + 1) * step], block) + dot(low[g * step : (g + 1) * step], block)
                )
            a = a + 0.9 * jnp.concatenate(parts, axis=0)
        v = forward_cols(jnp.where(span_mask(span, width), a, 0.0), csth, cstl)
        outs[s][...] = pack_halves(v, top).astype(outs[s].dtype)


def base_kernel(top, me_ref, picks_ref, v_ref, m_ref, acts_ref, ao1_ref, ao2_ref, g_ref, gp_ref, c4th_ref, c4tl_ref, csth_ref,
                cstl_ref, out_ref, a0_ref, sem):
    copy = fetch(me_ref, acts_ref, 0, 0, a0_ref, sem)
    copy.start()
    shard, width = m_ref.shape
    crows = shard // SIZE
    groups = crows // GROUP
    step = GROUP * top
    span, order = choice(picks_ref[...], top)
    hot = onehot(order)
    v = v_ref[...]
    parts = []
    for g in range(groups):
        block = v[g * step : (g + 1) * step]
        parts += [block[:, :SIZE], block[:, SIZE:]]
    vh, vl = split(jnp.concatenate(parts, axis=0))
    csth, cstl = csth_ref[...], cstl_ref[...]
    x = dot(vh, csth) + dot(vl, csth) + dot(vh, cstl)
    xh, xl = split(jnp.where(span_mask(span, width), x, 0.0))
    gmat, gpmat = g_ref[...], gp_ref[...]
    copy.wait()
    rows = GROUP * SIZE
    own = (iota((rows, 2 * step), 0) // SIZE) == ((iota((rows, 2 * step), 1) // top) % GROUP)
    for g in range(groups):
        here = slice(g * 2 * step, (g + 1) * 2 * step)
        th = jnp.where(own, dot_nt(c4th_ref[...], hot[here]), 0.0).astype(BF16)
        tl = jnp.where(own, dot_nt(c4tl_ref[...], hot[here]), 0.0).astype(BF16)
        inv = dot(th, xh[here]) + dot(tl, xh[here]) + dot(th, xl[here])
        at = slice(g * rows, (g + 1) * rows)
        ao_ref, first = (ao1_ref, 0) if 2 * g < groups else (ao2_ref, shard // 2)
        theirs = ao_ref[:, g * rows - first : (g + 1) * rows - first]
        pair = dot_tn(a0_ref[:, at], gmat) + dot_tn(theirs, gpmat)
        out_ref[at, :] = 0.9 * m_ref[at, :].astype(F32) + pair - inv


def update_kernel(top, crows, pack_ref, c2th_ref, c2tl_ref, csth_ref, cstl_ref, after_ref, out_ref, xh_ref, xl_ref):
    del after_ref
    reps = pack_ref.shape[0]
    width = out_ref.shape[1]
    per = crows * top

    @pl.when(pl.program_id(0) == 0)
    def _():
        out_ref[...] = jnp.zeros_like(out_ref)

    r1 = iota((per, crows), 0)
    spread = (iota((per, crows), 1) == r1 // top).astype(F32).astype(BF16)
    pickmask = iota((per, LANES), 1) == iota((per, LANES), 0) % top
    csth, cstl = csth_ref[...], cstl_ref[...]
    zero = jnp.zeros_like(csth)
    numbers = []
    for r in range(reps):
        v = pack_ref[r, :per, :]
        picks = pack_ref[r, per : per + crows, :]
        number = jnp.sum(jnp.where(pickmask, dot(spread, picks), 0.0), axis=1, keepdims=True).astype(jnp.int32)
        numbers.append(number)
        mask = span_mask(number // (SIZE // 2), width)
        for p in range(2):
            wh = jnp.concatenate([csth, zero] if p == 0 else [zero, csth], axis=0)
            wl = jnp.concatenate([cstl, zero] if p == 0 else [zero, cstl], axis=0)
            xh, xl = split(jnp.where(mask, dot(v, wh) + dot(v, wl), 0.0))
            xh_ref[p, r] = xh
            xl_ref[p, r] = xl
    pair = 2 * top
    cols = 2 * reps * pair
    rows = 2 * SIZE
    own = (iota((rows, cols), 0) // SIZE) == ((iota((rows, cols), 1) // top) % 2)
    for g in range(crows // 2):
        at = slice(g * pair, (g + 1) * pair)
        bh = jnp.concatenate([xh_ref[p, r, at, :] for p in range(2) for r in range(reps)], axis=0)
        bl = jnp.concatenate([xl_ref[p, r, at, :] for p in range(2) for r in range(reps)], axis=0)
        order = jnp.concatenate(
            [2 * (numbers[r][at] % (SIZE // 2)) + p for p in range(2) for r in range(reps)], axis=0
        )
        hot = onehot(order)
        th = jnp.where(own, dot_nt(c2th_ref[...], hot), 0.0).astype(BF16)
        tl = jnp.where(own, dot_nt(c2tl_ref[...], hot), 0.0).astype(BF16)
        out_ref[g * rows : (g + 1) * rows, :] += dot(th, bh) + dot(tl, bh) + dot(th, bl)


def fetch(me_ref, acts_ref, s, start, cols, sem):
    shard = acts_ref.shape[1] // 4
    at = pl.multiple_of((me_ref[0] ^ s) * shard + start, LANES)
    return pltpu.make_async_copy(acts_ref.at[:, pl.ds(at, cols.shape[1])], cols, sem)


def cut_kernel(cuts, me_ref, acts_ref, after_ref, after2_ref, after3_ref, out_ref, sems):
    del after_ref, after2_ref, after3_ref
    shard = acts_ref.shape[1] // 4
    copies, to = [], 0
    for n, (s, start, size) in enumerate(cuts):
        at = pl.multiple_of((me_ref[0] ^ s) * shard + start, LANES)
        copies.append(
            pltpu.make_async_copy(acts_ref.at[:, pl.ds(at, size)], out_ref.at[:, to : to + size], sems.at[n])
        )
        to += size
    for copy in copies:
        copy.start()
    for copy in copies:
        copy.wait()


def sum_kernel(start, me_ref, acts_ref, g_ref, gp_ref, theirs_ref, after_ref, out_ref, cols, sem):
    del after_ref
    copy = fetch(me_ref, acts_ref, 2, start, cols, sem)
    copy.start()
    part = dot_tn(theirs_ref[...], gp_ref[...])
    copy.wait()
    out_ref[...] = (part + dot_tn(cols[...], g_ref[...])).astype(BF16)


def hold_kernel(x_ref, after_ref, after2_ref, out_ref):
    del x_ref, after_ref, after2_ref, out_ref


def early_kernel(base_ref, got1_ref, got2_ref, out_ref, rows, sems):
    copies, at = [], 0
    for n, got_ref in enumerate((got1_ref, got2_ref)):
        here = slice(at, at + got_ref.shape[0])
        rows[here, :] = (base_ref[here, :] + got_ref[...].astype(F32)).astype(BF16)
        copies.append(pltpu.make_async_copy(rows.at[here], out_ref.at[here], sems.at[n]))
        copies[-1].start()
        at += got_ref.shape[0]
    for copy in copies:
        copy.wait()


def last_kernel(base_ref, got_ref, early_ref, out_ref, rows, sems):
    del early_ref
    shard = base_ref.shape[0]
    size = got_ref.shape[0] // 3
    copies = []
    for n in range(3):
        here = slice(n * size, (n + 1) * size)
        there = slice(shard - (3 - n) * size, shard - (2 - n) * size)
        rows[here, :] = (base_ref[there, :] + got_ref[here, :].astype(F32)).astype(BF16)
        copies.append(pltpu.make_async_copy(rows.at[here], out_ref.at[there], sems.at[n]))
        copies[-1].start()
    for copy in copies:
        copy.wait()


def pack_kernel(own_ref, got1_ref, got2_ref, got3_ref, picks_ref, after_ref, values_ref, pack_ref):
    del after_ref
    count = own_ref.shape[0]
    values = own_ref[...] + got1_ref[...].astype(F32) + got2_ref[...].astype(F32) + got3_ref[...].astype(F32)
    values_ref[...] = values
    pack_ref[:count, :] = values.astype(BF16)
    pack_ref[count:, :] = picks_ref[...]


VMEM = functools.partial(pl.BlockSpec, memory_space=pltpu.VMEM)
SMEM = pl.BlockSpec(memory_space=pltpu.SMEM)
ANY = pl.BlockSpec(memory_space=pl.ANY)
HBM = pl.BlockSpec(memory_space=pltpu.HBM)
COST = pl.CostEstimate(flops=1, bytes_accessed=1, transcendentals=0)
PARAMS = pltpu.CompilerParams(vmem_limit_bytes=32 * 1024 * 1024)


def swap(x, bit, axis, size):
    return lax.ppermute(x, axis, [(i, i ^ bit) for i in range(size)])


def gather_replicas(x, replicas):
    if GATHER or replicas & (replicas - 1):
        return lax.all_gather(x, "replica", axis=0, tiled=False)
    stack, bit = x[None], 1
    while bit < replicas:
        stack = jnp.concatenate([stack, swap(stack, bit, "replica", replicas)], axis=0)
        bit *= 2
    return stack


def body(replicas, fsdp, activations, output_grads, momentum, chosen_blocks):
    old = momentum[0]
    shard, width = old.shape
    tokens = activations.shape[0]
    crows = shard // SIZE
    top = chosen_blocks.shape[2]
    lead = shard // 4
    second = SECOND
    spans = width // SIZE
    high, low = table_parts()
    c4h, c4l = (np.tile(t, (1, GROUP)) for t in (high, low))
    c4th, c4tl = (np.tile(t.T, (GROUP, 1)) for t in (high, low))
    c2th, c2tl = (np.tile(t.T, (2, 1)) for t in (high, low))
    csth, cstl = (np.tile(t, (1, spans)) for t in (high, low))
    me = lax.axis_index("fsdp")

    mine = jnp.reshape(me, (1,))
    picks = jnp.pad(chosen_blocks[0].astype(BF16), ((0, 0), (0, LANES - top)))
    count = crows * top

    def swap_near(x, bit):
        return swap(x, bit, "fsdp", fsdp)

    def call(kernel, name, outs, args, specs, cols=0):
        scratch = [pltpu.VMEM((tokens, cols), BF16), pltpu.SemaphoreType.DMA] if cols else []
        return pl.pallas_call(
            kernel,
            out_shape=outs,
            in_specs=[{"s": SMEM, "a": ANY, "h": HBM, "v": VMEM()}[c] for c in specs],
            out_specs=jax.tree.map(lambda _: VMEM(), outs),
            scratch_shapes=scratch,
            compiler_params=PARAMS,
            cost_estimate=COST,
            name=name,
        )(*args)

    def cut(cuts, after, after2, after3):
        return pl.pallas_call(
            functools.partial(cut_kernel, cuts),
            out_shape=bf(tokens, sum(size for _, _, size in cuts)),
            in_specs=[SMEM, HBM, ANY, ANY, ANY],
            out_specs=ANY,
            scratch_shapes=[pltpu.SemaphoreType.DMA((len(cuts),))],
            compiler_params=PARAMS,
            cost_estimate=COST,
            name="cut",
        )(mine, activations, after, after2, after3)

    def bf(*shape):
        return jax.ShapeDtypeStruct(shape, BF16)

    def f32(*shape):
        return jax.ShapeDtypeStruct(shape, F32)

    acts, grads = activations, output_grads
    got_picks = [swap_near(picks, s) for s in (1, 2, 3)]
    got_grads = swap_near(grads, 1)
    cols_1 = swap_near(cut([(3, 0, lead)], picks, picks, picks), 1)

    def sums(start, cols, after, name):
        size = cols.shape[1]
        kernel = functools.partial(sum_kernel, start)
        return call(kernel, name, bf(size, width), (mine, acts, grads, got_grads, cols, after), "shvvva", size)

    sum_1 = sums(0, cols_1, cols_1, "sum_1")
    got_1 = swap_near(sum_1, 2)
    picks4 = jnp.concatenate([picks, *got_picks], axis=0)
    cut_2 = cut([(3, lead, second)], picks4, cols_1, got_grads)
    cols_2 = swap_near(cut_2, 1)
    def hold(x, after, after2):
        return pl.pallas_call(
            hold_kernel,
            out_shape=bf(*x.shape),
            in_specs=[ANY] * 3,
            out_specs=ANY,
            input_output_aliases={0: 0},
            compiler_params=PARAMS,
            cost_estimate=COST,
            name="hold",
        )(x, after, after2)

    own, *parts = call(
        functools.partial(chosen_kernel, top),
        "chosen",
        [f32(count, 2 * SIZE)] + [bf(count, 2 * SIZE)] * 3,
        (mine, picks4, acts, grads, old, c4h, c4l, csth, cstl, sum_1),
        "s" + "v" * 8 + "a",
    )
    got = [swap_near(x, s + 1) for s, x in enumerate(parts)]
    sum_2 = sums(lead, cols_2, parts[0], "sum_2")
    sum_2 = hold(sum_2, got_1, got_1)
    values, pack = call(
        pack_kernel, "pack", [f32(count, 2 * SIZE), bf(count + crows, 2 * SIZE)], (own, *got, picks, sum_2), "vvvvva"
    )
    sum_2 = hold(sum_2, got_1, values)
    got_2 = swap_near(sum_2, 2)
    cols_3 = swap_near(cut([(3, lead + second, shard - lead - second)], values, values, values), 1)
    sum_3 = sums(lead + second, cols_3, sum_2, "sum_3")
    got_3 = swap_near(sum_3, 2)
    cols_own = [
        swap_near(cut([(1, n * (shard // 2), shard // 2)], sum_3, sum_3, sum_3), 1) for n in range(2)
    ]
    base = call(
        functools.partial(base_kernel, top),
        "base",
        f32(shard, width),
        (mine, picks, values, old, acts, *cols_own, grads, got_grads, c4th, c4tl, csth, cstl),
        "svvvhvvvvvvvv",
        shard,
    )

    everyone = gather_replicas(pack, replicas)
    step = 8 if replicas % 8 == 0 else 1
    update = pl.pallas_call(
        functools.partial(update_kernel, top, crows),
        grid=(replicas // step,),
        out_shape=jax.ShapeDtypeStruct((shard, width), F32),
        in_specs=[pl.BlockSpec((step, pack.shape[0], LANES), lambda i: (i, 0, 0))] + [VMEM()] * 4 + [ANY],
        out_specs=pl.BlockSpec((shard, width), lambda i: (0, 0)),
        scratch_shapes=[pltpu.VMEM((2, step, crows * top, width), BF16)] * 2,
        compiler_params=PARAMS,
        cost_estimate=COST,
        name="update",
    )(everyone, c2th, c2tl, csth, cstl, values)
    early = pl.pallas_call(
        early_kernel,
        out_shape=bf(shard, width),
        in_specs=[VMEM()] * 3,
        out_specs=HBM,
        scratch_shapes=[pltpu.VMEM((lead + second, width), BF16), pltpu.SemaphoreType.DMA((2,))],
        compiler_params=PARAMS,
        cost_estimate=COST,
        name="early",
    )(base, got_1, got_2)
    moment_next = pl.pallas_call(
        last_kernel,
        out_shape=bf(shard, width),
        in_specs=[VMEM(), VMEM(), HBM],
        out_specs=HBM,
        scratch_shapes=[pltpu.VMEM((shard - lead - second, width), BF16), pltpu.SemaphoreType.DMA((3,))],
        input_output_aliases={2: 0},
        compiler_params=PARAMS,
        cost_estimate=COST,
        name="last",
    )(base, got_3, early)
    return moment_next[None], update


def solution(mesh):
    return jax.shard_map(
        functools.partial(body, mesh.shape["replica"], mesh.shape["fsdp"]),
        mesh=mesh,
        in_specs=(
            P(("replica", "fsdp"), None),
            P(("replica", "fsdp"), None),
            P("replica", "fsdp", None),
            P("replica", "fsdp", None),
        ),
        out_specs=(P("replica", "fsdp", None), P("fsdp", None)),
        check_vma=False,
    )
```

```python
import functools

import jax
import jax.numpy as jnp
import numpy as np
from jax import lax
from jax.experimental import pallas as pl
from jax.experimental.pallas import tpu as pltpu
from jax.sharding import PartitionSpec as P

F32 = jnp.float32
BF16 = jnp.bfloat16
SIZE = 64
LANES = 128
GATHER = True
SECOND = 384
GROUP = 4


def table_parts():
    order = np.arange(SIZE, dtype=np.float64)[:, None]
    place = np.arange(SIZE, dtype=np.float64)[None, :]
    factor = np.where(order == 0, np.sqrt(1.0 / SIZE), np.sqrt(2.0 / SIZE))
    table = factor * np.cos(np.pi * (2 * place + 1) * order / (2 * SIZE))
    high = table.astype(jnp.bfloat16)
    low = (table - high.astype(np.float64)).astype(jnp.bfloat16)
    return high, low


def dot(a, b):
    return lax.dot_general(a, b, (((1,), (0,)), ((), ())), preferred_element_type=F32)


def dot_nt(a, b):
    return lax.dot_general(a, b, (((1,), (1,)), ((), ())), preferred_element_type=F32)


def dot_tn(a, b):
    return lax.dot_general(a, b, (((0,), (0,)), ((), ())), preferred_element_type=F32)


def split(x):
    high = x.astype(BF16)
    return high, (x - high.astype(F32)).astype(BF16)


def iota(shape, dim):
    return lax.broadcasted_iota(jnp.int32, shape, dim)


def choice(picks, top):
    crows = picks.shape[0]
    rows = crows * top * 2
    r1 = iota((rows, crows), 0)
    owner = GROUP * (r1 // (2 * GROUP * top)) + (r1 // top) % GROUP
    spread = (iota((rows, crows), 1) == owner).astype(F32).astype(BF16)
    r2 = iota((rows, LANES), 0)
    numbers = jnp.where(iota((rows, LANES), 1) == r2 % top, dot(spread, picks), 0.0)
    number = jnp.sum(numbers, axis=1, keepdims=True).astype(jnp.int32)
    half = (iota((rows, 1), 0) // (GROUP * top)) % 2
    return number // (SIZE // 2), 2 * (number % (SIZE // 2)) + half


def onehot(order):
    rows = order.shape[0]
    return (iota((rows, SIZE), 1) == order).astype(F32).astype(BF16)


def chosen_rows(order, top, c4h, c4l):
    rows = order.shape[0]
    hot = onehot(order)
    own = (iota((rows, GROUP * SIZE), 1) // SIZE) == ((iota((rows, GROUP * SIZE), 0) // top) % GROUP)
    high = jnp.where(own, dot(hot, c4h), 0.0).astype(BF16)
    low = jnp.where(own, dot(hot, c4l), 0.0).astype(BF16)
    return high, low


def span_mask(span, width):
    rows = span.shape[0]
    return (iota((rows, width), 1) // SIZE) == span


def forward_cols(masked, csth, cstl):
    high, low = split(masked)
    return dot_nt(high, csth) + dot_nt(low, csth) + dot_nt(high, cstl)


def pack_halves(v, top):
    step = GROUP * top
    parts = []
    for g in range(v.shape[0] // (2 * step)):
        a = v[2 * g * step : (2 * g + 1) * step]
        b = v[(2 * g + 1) * step : (2 * g + 2) * step]
        parts.append(jnp.concatenate([a, b], axis=1))
    return jnp.concatenate(parts, axis=0)


def chosen_kernel(top, me_ref, picks_ref, acts_ref, g_ref, m_ref, c4h_ref, c4l_ref, csth_ref, cstl_ref,
                  after_ref, *outs):
    del after_ref
    me = me_ref[0]
    shard = m_ref.shape[0]
    width = m_ref.shape[1]
    crows = shard // SIZE
    groups = crows // GROUP
    c4h, c4l = c4h_ref[...], c4l_ref[...]
    csth, cstl = csth_ref[...], cstl_ref[...]
    gmat = g_ref[...]
    for s in range(4):
        target = me ^ s
        span, order = choice(picks_ref[s * crows : (s + 1) * crows, :], top)
        high, low = chosen_rows(order, top, c4h, c4l)
        step = 2 * GROUP * top
        parts = []
        for g in range(groups):
            start = pl.multiple_of(target * shard + g * GROUP * SIZE, GROUP * SIZE)
            block = acts_ref[:, pl.ds(start, GROUP * SIZE)]
            both = jnp.concatenate([high[g * step : (g + 1) * step], low[g * step : (g + 1) * step]], axis=0)
            t = dot_nt(both, block)
            parts.append(t[:step] + t[step:])
        th, tl = split(jnp.concatenate(parts, axis=0))
        a = dot(th, gmat) + dot(tl, gmat)
        if s == 0:
            parts = []
            for g in range(groups):
                block = m_ref[g * GROUP * SIZE : (g + 1) * GROUP * SIZE, :]
                parts.append(
                    dot(high[g * step : (g + 1) * step], block) + dot(low[g * step : (g + 1) * step], block)
                )
            a = a + 0.9 * jnp.concatenate(parts, axis=0)
        v = forward_cols(jnp.where(span_mask(span, width), a, 0.0), csth, cstl)
        outs[s][...] = pack_halves(v, top).astype(outs[s].dtype)


def base_kernel(top, me_ref, picks_ref, v_ref, m_ref, acts_ref, ao1_ref, ao2_ref, g_ref, gp_ref, c4th_ref, c4tl_ref, csth_ref,
                cstl_ref, out_ref, a0_ref, sem):
    copy = fetch(me_ref, acts_ref, 0, 0, a0_ref, sem)
    copy.start()
    shard, width = m_ref.shape
    crows = shard // SIZE
    groups = crows // GROUP
    step = GROUP * top
    span, order = choice(picks_ref[...], top)
    hot = onehot(order)
    v = v_ref[...]
    parts = []
    for g in range(groups):
        block = v[g * step : (g + 1) * step]
        parts += [block[:, :SIZE], block[:, SIZE:]]
    vh, vl = split(jnp.concatenate(parts, axis=0))
    csth, cstl = csth_ref[...], cstl_ref[...]
    x = dot(vh, csth) + dot(vl, csth) + dot(vh, cstl)
    xh, xl = split(jnp.where(span_mask(span, width), x, 0.0))
    gmat, gpmat = g_ref[...], gp_ref[...]
    copy.wait()
    rows = GROUP * SIZE
    own = (iota((rows, 2 * step), 0) // SIZE) == ((iota((rows, 2 * step), 1) // top) % GROUP)
    for g in range(groups):
        here = slice(g * 2 * step, (g + 1) * 2 * step)
        th = jnp.where(own, dot_nt(c4th_ref[...], hot[here]), 0.0).astype(BF16)
        tl = jnp.where(own, dot_nt(c4tl_ref[...], hot[here]), 0.0).astype(BF16)
        inv = dot(th, xh[here]) + dot(tl, xh[here]) + dot(th, xl[here])
        at = slice(g * rows, (g + 1) * rows)
        ao_ref, first = (ao1_ref, 0) if 2 * g < groups else (ao2_ref, shard // 2)
        theirs = ao_ref[:, g * rows - first : (g + 1) * rows - first]
        pair = dot_tn(a0_ref[:, at], gmat) + dot_tn(theirs, gpmat)
        out_ref[at, :] = 0.9 * m_ref[at, :].astype(F32) + pair - inv


def update_kernel(top, crows, pack_ref, c2th_ref, c2tl_ref, csth_ref, cstl_ref, after_ref, out_ref, xh_ref, xl_ref):
    del after_ref
    reps = pack_ref.shape[0]
    width = out_ref.shape[1]
    per = crows * top

    @pl.when(pl.program_id(0) == 0)
    def _():
        out_ref[...] = jnp.zeros_like(out_ref)

    r1 = iota((per, crows), 0)
    spread = (iota((per, crows), 1) == r1 // top).astype(F32).astype(BF16)
    pickmask = iota((per, LANES), 1) == iota((per, LANES), 0) % top
    csth, cstl = csth_ref[...], cstl_ref[...]
    zero = jnp.zeros_like(csth)
    numbers = []
    for r in range(reps):
        v = pack_ref[r, :per, :]
        picks = pack_ref[r, per : per + crows, :]
        number = jnp.sum(jnp.where(pickmask, dot(spread, picks), 0.0), axis=1, keepdims=True).astype(jnp.int32)
        numbers.append(number)
        mask = span_mask(number // (SIZE // 2), width)
        for p in range(2):
            wh = jnp.concatenate([csth, zero] if p == 0 else [zero, csth], axis=0)
            wl = jnp.concatenate([cstl, zero] if p == 0 else [zero, cstl], axis=0)
            xh, xl = split(jnp.where(mask, dot(v, wh) + dot(v, wl), 0.0))
            xh_ref[p, r] = xh
            xl_ref[p, r] = xl
    pair = 2 * top
    cols = 2 * reps * pair
    rows = 2 * SIZE
    own = (iota((rows, cols), 0) // SIZE) == ((iota((rows, cols), 1) // top) % 2)
    for g in range(crows // 2):
        at = slice(g * pair, (g + 1) * pair)
        bh = jnp.concatenate([xh_ref[p, r, at, :] for p in range(2) for r in range(reps)], axis=0)
        bl = jnp.concatenate([xl_ref[p, r, at, :] for p in range(2) for r in range(reps)], axis=0)
        order = jnp.concatenate(
            [2 * (numbers[r][at] % (SIZE // 2)) + p for p in range(2) for r in range(reps)], axis=0
        )
        hot = onehot(order)
        th = jnp.where(own, dot_nt(c2th_ref[...], hot), 0.0).astype(BF16)
        tl = jnp.where(own, dot_nt(c2tl_ref[...], hot), 0.0).astype(BF16)
        out_ref[g * rows : (g + 1) * rows, :] += dot(th, bh) + dot(tl, bh) + dot(th, bl)


def fetch(me_ref, acts_ref, s, start, cols, sem):
    shard = acts_ref.shape[1] // 4
    at = pl.multiple_of((me_ref[0] ^ s) * shard + start, LANES)
    return pltpu.make_async_copy(acts_ref.at[:, pl.ds(at, cols.shape[1])], cols, sem)


def cut_kernel(cuts, me_ref, acts_ref, after_ref, after2_ref, after3_ref, out_ref, sems):
    del after_ref, after2_ref, after3_ref
    shard = acts_ref.shape[1] // 4
    copies, to = [], 0
    for n, (s, start, size) in enumerate(cuts):
        at = pl.multiple_of((me_ref[0] ^ s) * shard + start, LANES)
        copies.append(
            pltpu.make_async_copy(acts_ref.at[:, pl.ds(at, size)], out_ref.at[:, to : to + size], sems.at[n])
        )
        to += size
    for copy in copies:
        copy.start()
    for copy in copies:
        copy.wait()


def sum_kernel(start, me_ref, acts_ref, g_ref, gp_ref, theirs_ref, after_ref, out_ref, cols, sem):
    del after_ref
    copy = fetch(me_ref, acts_ref, 2, start, cols, sem)
    copy.start()
    part = dot_tn(theirs_ref[...], gp_ref[...])
    copy.wait()
    out_ref[...] = (part + dot_tn(cols[...], g_ref[...])).astype(BF16)


def hold_kernel(x_ref, after_ref, after2_ref, out_ref):
    del x_ref, after_ref, after2_ref, out_ref


def early_kernel(base_ref, got1_ref, got2_ref, out_ref, rows, sems):
    copies, at = [], 0
    for n, got_ref in enumerate((got1_ref, got2_ref)):
        here = slice(at, at + got_ref.shape[0])
        rows[here, :] = (base_ref[here, :] + got_ref[...].astype(F32)).astype(BF16)
        copies.append(pltpu.make_async_copy(rows.at[here], out_ref.at[here], sems.at[n]))
        copies[-1].start()
        at += got_ref.shape[0]
    for copy in copies:
        copy.wait()


def last_kernel(base_ref, got_ref, early_ref, out_ref, rows, sems):
    del early_ref
    shard = base_ref.shape[0]
    size = got_ref.shape[0] // 2
    copies = []
    for n in range(2):
        here = slice(n * size, (n + 1) * size)
        there = slice(shard - (2 - n) * size, shard - (1 - n) * size)
        rows[here, :] = (base_ref[there, :] + got_ref[here, :].astype(F32)).astype(BF16)
        copies.append(pltpu.make_async_copy(rows.at[here], out_ref.at[there], sems.at[n]))
        copies[-1].start()
    for copy in copies:
        copy.wait()


def pack_kernel(own_ref, got1_ref, got2_ref, got3_ref, picks_ref, after_ref, values_ref, pack_ref):
    del after_ref
    count = own_ref.shape[0]
    values = own_ref[...] + got1_ref[...].astype(F32) + got2_ref[...].astype(F32) + got3_ref[...].astype(F32)
    values_ref[...] = values
    pack_ref[:count, :] = values.astype(BF16)
    pack_ref[count:, :] = picks_ref[...]


VMEM = functools.partial(pl.BlockSpec, memory_space=pltpu.VMEM)
SMEM = pl.BlockSpec(memory_space=pltpu.SMEM)
ANY = pl.BlockSpec(memory_space=pl.ANY)
HBM = pl.BlockSpec(memory_space=pltpu.HBM)
COST = pl.CostEstimate(flops=1, bytes_accessed=1, transcendentals=0)
PARAMS = pltpu.CompilerParams(vmem_limit_bytes=32 * 1024 * 1024)


def swap(x, bit, axis, size):
    return lax.ppermute(x, axis, [(i, i ^ bit) for i in range(size)])


def gather_replicas(x, replicas):
    if GATHER or replicas & (replicas - 1):
        return lax.all_gather(x, "replica", axis=0, tiled=False)
    stack, bit = x[None], 1
    while bit < replicas:
        stack = jnp.concatenate([stack, swap(stack, bit, "replica", replicas)], axis=0)
        bit *= 2
    return stack


def body(replicas, fsdp, activations, output_grads, momentum, chosen_blocks):
    old = momentum[0]
    shard, width = old.shape
    tokens = activations.shape[0]
    crows = shard // SIZE
    top = chosen_blocks.shape[2]
    lead = shard // 4
    second = SECOND
    spans = width // SIZE
    high, low = table_parts()
    c4h, c4l = (np.tile(t, (1, GROUP)) for t in (high, low))
    c4th, c4tl = (np.tile(t.T, (GROUP, 1)) for t in (high, low))
    c2th, c2tl = (np.tile(t.T, (2, 1)) for t in (high, low))
    csth, cstl = (np.tile(t, (1, spans)) for t in (high, low))
    me = lax.axis_index("fsdp")

    mine = jnp.reshape(me, (1,))
    picks = jnp.pad(chosen_blocks[0].astype(BF16), ((0, 0), (0, LANES - top)))
    count = crows * top

    def swap_near(x, bit):
        return swap(x, bit, "fsdp", fsdp)

    def call(kernel, name, outs, args, specs, cols=0):
        scratch = [pltpu.VMEM((tokens, cols), BF16), pltpu.SemaphoreType.DMA] if cols else []
        return pl.pallas_call(
            kernel,
            out_shape=outs,
            in_specs=[{"s": SMEM, "a": ANY, "h": HBM, "v": VMEM()}[c] for c in specs],
            out_specs=jax.tree.map(lambda _: VMEM(), outs),
            scratch_shapes=scratch,
            compiler_params=PARAMS,
            cost_estimate=COST,
            name=name,
        )(*args)

    def cut(cuts, after, after2, after3):
        return pl.pallas_call(
            functools.partial(cut_kernel, cuts),
            out_shape=bf(tokens, sum(size for _, _, size in cuts)),
            in_specs=[SMEM, HBM, ANY, ANY, ANY],
            out_specs=ANY,
            scratch_shapes=[pltpu.SemaphoreType.DMA((len(cuts),))],
            compiler_params=PARAMS,
            cost_estimate=COST,
            name="cut",
        )(mine, activations, after, after2, after3)

    def bf(*shape):
        return jax.ShapeDtypeStruct(shape, BF16)

    def f32(*shape):
        return jax.ShapeDtypeStruct(shape, F32)

    acts, grads = activations, output_grads
    got_picks = [swap_near(picks, s) for s in (1, 2, 3)]
    got_grads = swap_near(grads, 1)
    cols_1 = swap_near(cut([(3, 0, lead)], picks, picks, picks), 1)

    def sums(start, cols, after, name):
        size = cols.shape[1]
        kernel = functools.partial(sum_kernel, start)
        return call(kernel, name, bf(size, width), (mine, acts, grads, got_grads, cols, after), "shvvva", size)

    sum_1 = sums(0, cols_1, cols_1, "sum_1")
    got_1 = swap_near(sum_1, 2)
    picks4 = jnp.concatenate([picks, *got_picks], axis=0)
    cut_2 = cut([(3, lead, second)], picks4, cols_1, got_grads)
    cols_2 = swap_near(cut_2, 1)
    own, *parts = call(
        functools.partial(chosen_kernel, top),
        "chosen",
        [f32(count, 2 * SIZE)] + [bf(count, 2 * SIZE)] * 3,
        (mine, picks4, acts, grads, old, c4h, c4l, csth, cstl, sum_1),
        "s" + "v" * 8 + "a",
    )
    got = [swap_near(x, s + 1) for s, x in enumerate(parts)]
    sum_2 = sums(lead, cols_2, got_1, "sum_2")
    values, pack = call(
        pack_kernel, "pack", [f32(count, 2 * SIZE), bf(count + crows, 2 * SIZE)], (own, *got, picks, sum_2), "vvvvva"
    )
    sum_2 = pl.pallas_call(
        hold_kernel,
        out_shape=bf(*sum_2.shape),
        in_specs=[ANY] * 3,
        out_specs=ANY,
        input_output_aliases={0: 0},
        compiler_params=PARAMS,
        cost_estimate=COST,
        name="hold",
    )(sum_2, got_1, values)
    got_2 = swap_near(sum_2, 2)
    cols_3 = swap_near(cut([(3, lead + second, shard - lead - second)], values, values, values), 1)
    sum_3 = sums(lead + second, cols_3, sum_2, "sum_3")
    got_3 = swap_near(sum_3, 2)
    cols_own = [
        swap_near(cut([(1, n * (shard // 2), shard // 2)], (sum_2, sum_3)[n], sum_2, sum_2), 1) for n in range(2)
    ]
    base = call(
        functools.partial(base_kernel, top),
        "base",
        f32(shard, width),
        (mine, picks, values, old, acts, *cols_own, grads, got_grads, c4th, c4tl, csth, cstl),
        "svvvhvvvvvvvv",
        shard,
    )

    everyone = gather_replicas(pack, replicas)
    step = 8 if replicas % 8 == 0 else 1
    update = pl.pallas_call(
        functools.partial(update_kernel, top, crows),
        grid=(replicas // step,),
        out_shape=jax.ShapeDtypeStruct((shard, width), F32),
        in_specs=[pl.BlockSpec((step, pack.shape[0], LANES), lambda i: (i, 0, 0))] + [VMEM()] * 4 + [ANY],
        out_specs=pl.BlockSpec((shard, width), lambda i: (0, 0)),
        scratch_shapes=[pltpu.VMEM((2, step, crows * top, width), BF16)] * 2,
        compiler_params=PARAMS,
        cost_estimate=COST,
        name="update",
    )(everyone, c2th, c2tl, csth, cstl, values)
    early = pl.pallas_call(
        early_kernel,
        out_shape=bf(shard, width),
        in_specs=[VMEM()] * 3,
        out_specs=HBM,
        scratch_shapes=[pltpu.VMEM((lead + second, width), BF16), pltpu.SemaphoreType.DMA((2,))],
        compiler_params=PARAMS,
        cost_estimate=COST,
        name="early",
    )(base, got_1, got_2)
    moment_next = pl.pallas_call(
        last_kernel,
        out_shape=bf(shard, width),
        in_specs=[VMEM(), VMEM(), HBM],
        out_specs=HBM,
        scratch_shapes=[pltpu.VMEM((shard - lead - second, width), BF16), pltpu.SemaphoreType.DMA((2,))],
        input_output_aliases={2: 0},
        compiler_params=PARAMS,
        cost_estimate=COST,
        name="last",
    )(base, got_3, early)
    return moment_next[None], update


def solution(mesh):
    return jax.shard_map(
        functools.partial(body, mesh.shape["replica"], mesh.shape["fsdp"]),
        mesh=mesh,
        in_specs=(
            P(("replica", "fsdp"), None),
            P(("replica", "fsdp"), None),
            P("replica", "fsdp", None),
            P("replica", "fsdp", None),
        ),
        out_specs=(P("replica", "fsdp", None), P("fsdp", None)),
        check_vma=False,
    )
```
